32 devices in a mesh: row: 8 (over z, x), feat: 4 (over y, core).
Axes of the slice: x: 2, y: 2, z: 4, core: 2. Of those that a mesh axis runs over, the one named last changes fastest.
Arguments:
- predictor: float32 [16384], P(('row', 'feat')), may hold values from -3 to 3
- events: int32 [16384], P(('row', 'feat')), may hold values 0 or 1
- tie_groups: int32 [16384], P(('row', 'feat')), may hold values from 7 to 16383, as said below
- node_ids: int32 [16384], P('row'), may hold values from 0 to 7
- bin_index: int32 [512, 16384], P('feat', 'row'), may hold values from 0 to 255
Outputs:
- gradient: float32 [16384], P(('row', 'feat'))
- hessian: float32 [16384], P(('row', 'feat'))
- split_gain: float32 [8, 512, 256], P(None, 'feat', 'row')
The draws below stay inside these ranges and needn't reach their ends.
Inputs may be any that keep to these rules, and one draw needn't show every extreme that they name: tie_groups never falls along the rows; each value names a run of 1 to 8 consecutive rows, some run has exactly 8, and a new run begins at every multiple of 8 rows.
All inputs are finite; a program needn't handle non-finite values. No bound on the sum of `events` on one device may be relied on, other than what follows from the above.
Results may differ from the reference program's by a relative error of at most 0.0003.
The reference program's roundings to bfloat16 on the way (of `stats`) count: a program that leaves them out, or rounds other values in their place, can miss the bound.
Values may be sent and summed in bfloat16 or wider, within the bound.
A program may use at most 64 MiB of HBM per device.

```python
import jax
import jax.numpy as jnp
from jax import lax

F = 512
BINS = 256
NODES = 8
TIE_MOST = 8
ROWS = 16384


def draw_tie_groups(key, part):
    row_index = jnp.arange(ROWS, dtype=jnp.int32)
    coin_flips = jax.random.randint(key, (ROWS,), 0, 3)
    begins = (coin_flips == 0) | (row_index % TIE_MOST == 0)
    begins = jnp.where(row_index < TIE_MOST, row_index == 0, begins)
    finish = jnp.concatenate([begins[1:], jnp.ones((1,), jnp.bool_)])
    return lax.cummin(jnp.where(finish, row_index, ROWS - 1), axis=0, reverse=True).astype(jnp.int32)


def set_ends(entries, stream_key, least, largest):
    shape = entries.shape
    place = [jax.random.randint(jax.random.fold_in(stream_key, axis), (), 0, shape[axis]) for axis in range(len(shape))]
    entries = entries.at[tuple(place)].set(least)
    longest = shape.index(max(shape))
    place[longest] = (place[longest] + 1) % shape[longest]
    return entries.at[tuple(place)].set(largest)


def level_of(stream_key, shape, shards, low, top_value):
    def one(position, blocks):
        steps = jax.random.uniform(jax.random.fold_in(jax.random.fold_in(stream_key, 6), position), (blocks,), jnp.float32, low / len(shards), top_value / len(shards))
        return jnp.repeat(jnp.exp(steps), shape[position] // blocks).reshape((-1,) + (1,) * (len(shape) - position - 1))

    level = one(*shards[0])
    for cut in shards[1:]:
        level = level * one(*cut)
    return level


def scatter_about(own_key, dims, scale, most, split=(), kind=jnp.bfloat16):
    drawn = scale * jax.random.normal(own_key, dims, jnp.float32)
    if split:
        drawn = drawn * level_of(own_key, dims, split, -0.22, 0.18)
    return jnp.clip(drawn, -most, most).astype(kind)


def setup_inputs(seed: int = 0) -> dict:
    seeds = jax.random.split(jax.random.key(seed), 6)
    predictor = scatter_about(seeds[0], (ROWS,), 0.5, 3.0, ((0, 32),), jnp.float32)
    events = set_ends((jax.random.randint(seeds[1], (ROWS,), 0, 2) < 1).astype(jnp.int32), jax.random.fold_in(seeds[1], 1), 0, 1)
    tie_groups = draw_tie_groups(jax.random.fold_in(seeds[5], 71), 0)
    node_ids = set_ends(jax.random.randint(seeds[3], (ROWS,), 0, NODES), jax.random.fold_in(seeds[3], 1), 0, NODES - 1).astype(jnp.int32)
    bin_index = set_ends(jax.random.randint(seeds[4], (F, ROWS), 0, BINS), jax.random.fold_in(seeds[4], 1), 0, BINS - 1).astype(jnp.int32)
    return {"predictor": predictor, "events": events, "tie_groups": tie_groups, "node_ids": node_ids, "bin_index": bin_index}


def group_bounds(tie_groups):
    length = tie_groups.shape[0]
    row_index = jnp.arange(length, dtype=jnp.int32)
    change = tie_groups[1:] != tie_groups[:-1]
    begins = jnp.concatenate([jnp.ones((1,), jnp.bool_), change])
    finish = jnp.concatenate([change, jnp.ones((1,), jnp.bool_)])
    first_row = lax.cummax(jnp.where(begins, row_index, 0), axis=0)
    last_row = lax.cummin(jnp.where(finish, row_index, length - 1), axis=0, reverse=True)
    return first_row, last_row


def reference(predictor, events, tie_groups, node_ids, bin_index):
    hazard_exp = jnp.exp(predictor)
    suffix = jnp.cumsum(hazard_exp[::-1])[::-1]
    first_row, last_row = group_bounds(tie_groups)
    risk_sum = suffix[first_row]
    failed = events.astype(jnp.float32)
    weight_one = failed / risk_sum
    weight_two = failed / (risk_sum * risk_sum)
    hazard_one = jnp.cumsum(weight_one)[last_row]
    hazard_two = jnp.cumsum(weight_two)[last_row]
    gradient = hazard_exp * hazard_one - failed
    hessian = hazard_exp * hazard_one - hazard_exp * hazard_exp * hazard_two
    rounded = lax.optimization_barrier(jnp.stack([gradient, hessian]).astype(jnp.bfloat16))
    stats = rounded.astype(jnp.float32).T

    def feature_hist(column):
        segment = node_ids * BINS + column
        summed = jax.ops.segment_sum(stats, segment, num_segments=NODES * BINS)
        return summed.reshape(NODES, BINS, 2).transpose(0, 2, 1)

    hist = lax.map(feature_hist, bin_index)
    left_sums = jnp.cumsum(hist, axis=3)
    totals = jnp.sum(hist, axis=3, keepdims=True)
    grad_left = left_sums[:, :, 0]
    hess_left = left_sums[:, :, 1]
    grad_all = totals[:, :, 0]
    hess_all = totals[:, :, 1]
    gain = (grad_left * grad_left / (hess_left + 1.0)
            + (grad_all - grad_left) ** 2 / (hess_all - hess_left + 1.0)
            - grad_all * grad_all / (hess_all + 1.0))
    return gradient, hessian, gain.transpose(1, 0, 2)
```

```python
import functools

import jax
import jax.numpy as jnp
from jax import lax
from jax.experimental import pallas as pl
from jax.experimental.pallas import tpu as pltpu
from jax.sharding import PartitionSpec as P

BINS = 256
NODES = 8
LANES = 128
HIGH = 4
LOW = BINS // HIGH
CHANNELS = 2 * NODES
GROUP = 4
BLOCKS = 4
MESH = pl.DeviceIdType.MESH
EXACT = lax.Precision.HIGHEST


def partner(me, step, count):
    other = me
    bit = 1
    while bit < count:
        other = other + ((step // bit) % 2) * bit * (1 - 2 * ((me // bit) % 2))
        bit *= 2
    return other


def triangle(rows, columns, keep):
    a = lax.broadcasted_iota(jnp.int32, (rows, columns), 0)
    b = lax.broadcasted_iota(jnp.int32, (rows, columns), 1)
    return keep(a, b).astype(jnp.float32)


def exact_dot(a, b):
    return jnp.dot(a, b, precision=EXACT, preferred_element_type=jnp.float32)


def fill(value, known, step):
    for distance in (1, 2, 4):
        shift = distance if step > 0 else LANES - distance
        value = jnp.where(known > 0, value, pltpu.roll(value, shift, 1))
        known = jnp.maximum(known, pltpu.roll(known, shift, 1))
    return value


def cox(score, code):
    rows = score.shape[0]
    hazard_exp = jnp.exp(score)
    tie = code // 2
    failed = (code - 2 * tie).astype(jnp.float32)
    lane = lax.broadcasted_iota(jnp.int32, (rows, LANES), 1)
    begins = ((lane % 8 == 0) | (tie != pltpu.roll(tie, 1, 1))).astype(jnp.float32)
    finish = pltpu.roll(begins, LANES - 1, 1)
    lane_suffix = exact_dot(hazard_exp, triangle(LANES, LANES, lambda a, b: a >= b))
    whole = jnp.broadcast_to(lane_suffix[:, :1], (rows, LANES))
    suffix = lane_suffix + exact_dot(triangle(rows, rows, lambda a, b: b > a), whole)
    risk_sum = fill(suffix, begins, 1)
    weight_one = failed / risk_sum
    weight_two = failed / (risk_sum * risk_sum)
    upper = triangle(LANES, LANES, lambda a, b: a <= b)
    earlier = triangle(rows, rows, lambda a, b: b < a)

    def running(weight):
        within = exact_dot(weight, upper)
        whole = jnp.broadcast_to(within[:, LANES - 1 :], (rows, LANES))
        return fill(within + exact_dot(earlier, whole), finish, -1)

    hazard_one = running(weight_one)
    hazard_two = running(weight_two)
    gradient = hazard_exp * hazard_one - failed
    hessian = hazard_exp * hazard_one - hazard_exp * hazard_exp * hazard_two
    return gradient, hessian


def kernel(
    nr, nf, pred_ref, event_ref, tie_ref, node_ref, bin_ref, grad_ref, hess_ref, gain_ref,
    pay, nodes, bin_send, bin_recv, gain_send, gain_recv, acc, turned, score, code, grads, hesss,
    levelled, pay_send_sem, pay_sem, node_send_sem, node_sem, bin_send_sem, bin_sem, gain_send_sem, gain_sem,
):
    my_row = lax.axis_index("row")
    my_feat = lax.axis_index("feat")
    me = my_row * nf + my_feat
    count = nr * nf
    quarter = pred_ref.shape[0]
    blocks = bin_ref.shape[1] // LANES
    own = bin_ref.shape[0] // nr
    tile = bin_send.shape[2]
    slice_bins = BINS // nr

    def coords(device):
        return (device // nf, device % nf)

    barrier = pltpu.get_barrier_semaphore()

    def greet(step, carry):
        other = (me + step) % count
        pl.semaphore_signal(barrier, inc=1, device_id=coords(other), device_id_type=MESH)
        return carry

    lax.fori_loop(1, count, greet, 0)

    pay[me, 0:quarter, :] = pred_ref[...]
    pay[me, quarter : 2 * quarter, :] = (tie_ref[...] * 2 + event_ref[...]).astype(jnp.float32)
    nodes[my_row] = node_ref[...].astype(jnp.float32).astype(jnp.bfloat16)

    def pack(block, carry):
        lanes = pl.ds(pl.multiple_of(block * LANES, LANES), LANES)
        for target in range(nr):
            part = bin_ref[target * own : (target + 1) * own, lanes].astype(jnp.float32)
            if own < tile:
                part = jnp.concatenate([part, jnp.zeros((tile - own, LANES), jnp.float32)], axis=0)
            bin_send[target, block] = part.astype(jnp.bfloat16)
        return carry

    lax.fori_loop(0, blocks, pack, 0)
    pl.semaphore_wait(barrier, count - 1)

    def pay_copy(other):
        return pltpu.make_async_remote_copy(
            src_ref=pay.at[me], dst_ref=pay.at[me], send_sem=pay_send_sem, recv_sem=pay_sem,
            device_id=coords(other), device_id_type=MESH,
        )

    def node_copy(step):
        other = partner(my_row, step, nr)
        return pltpu.make_async_remote_copy(
            src_ref=nodes.at[my_row], dst_ref=nodes.at[my_row],
            send_sem=node_send_sem, recv_sem=node_sem,
            device_id=(other, my_feat), device_id_type=MESH,
        )

    def bin_copy(step):
        other = partner(my_row, step, nr)
        return pltpu.make_async_remote_copy(
            src_ref=bin_send.at[other], dst_ref=bin_recv.at[my_row],
            send_sem=bin_send_sem.at[step], recv_sem=bin_sem.at[step],
            device_id=(other, my_feat), device_id_type=MESH,
        )

    def gain_copy(step):
        other = partner(my_row, step, nr)
        return pltpu.make_async_remote_copy(
            src_ref=gain_send.at[other], dst_ref=gain_recv.at[my_row],
            send_sem=gain_send_sem.at[step], recv_sem=gain_sem.at[step],
            device_id=(other, my_feat), device_id_type=MESH,
        )

    def send_pay(step, carry):
        pay_copy((me + step) % count).start()
        return carry

    lax.fori_loop(1, count, send_pay, 0)

    def send_nodes(step, carry):
        node_copy(step).start()
        return carry

    lax.fori_loop(1, nr, send_nodes, 0)

    def send_bins(step, carry):
        bin_copy(nr - step).start()
        return carry

    lax.fori_loop(1, nr, send_bins, 0)

    bin_recv[my_row] = bin_send[my_row]
    acc[...] = jnp.zeros_like(acc)

    others = pl.ds(0, count - 1)
    pltpu.make_async_copy(pay.at[others], pay.at[others], pay_sem).wait()

    def spread(device, carry):
        rows = pl.ds(device * quarter, quarter)
        score[rows, :] = pay[device, 0:quarter, :]
        code[rows, :] = pay[device, quarter : 2 * quarter, :].astype(jnp.int32)
        return carry

    lax.fori_loop(0, count, spread, 0)
    gradient, hessian = cox(score[...], code[...])
    grads[...] = gradient
    hesss[...] = hessian
    mine = pl.ds(me * quarter, quarter)
    grad_ref[...] = grads[mine, :]
    hess_ref[...] = hesss[mine, :]

    row_others = pl.ds(0, nr - 1)
    pltpu.make_async_copy(nodes.at[row_others], nodes.at[row_others], node_sem).wait()
    for source in range(nr):
        levelled[source * blocks : (source + 1) * blocks, :] = nodes[source].astype(jnp.float32)

    levels = lax.broadcasted_iota(jnp.int32, (NODES, LANES), 0).astype(jnp.float32)
    low_levels = [
        (lax.broadcasted_iota(jnp.int32, (16, LANES), 0) + 16 * part).astype(jnp.float32).astype(jnp.bfloat16)
        for part in range(LOW // 16)
    ]
    one = jnp.ones((16, LANES), jnp.bfloat16)
    zero = jnp.zeros((16, LANES), jnp.bfloat16)
    groups = -(-own // GROUP)

    def one_source(step, carry):
        source = partner(my_row, step, nr)

        @pl.when(step > 0)
        def _():
            bin_copy(step).wait_recv()

        def one_chunk(chunk, carry):
            weights, highs, lows = [], [], []
            for inner in range(BLOCKS):
                block = chunk * BLOCKS + inner
                row = pl.ds(source * blocks + block, 1)
                is_node = jnp.broadcast_to(levelled[row, :], (NODES, LANES)) == levels
                weight = jnp.concatenate(
                    [
                        jnp.where(is_node, jnp.broadcast_to(grads[row, :], (NODES, LANES)), 0.0),
                        jnp.where(is_node, jnp.broadcast_to(hesss[row, :], (NODES, LANES)), 0.0),
                    ],
                    axis=0,
                )
                weights.append(weight.astype(jnp.bfloat16))
                bins = bin_recv[source, block].astype(jnp.float32)
                high = jnp.floor(bins * (1.0 / LOW))
                highs.append(high)
                lows.append(bins - high * LOW)
            for group in range(groups):
                left, right = [], []
                for inner in range(GROUP):
                    feature = group * GROUP + inner
                    high = [jnp.broadcast_to(h[feature : feature + 1], (16, LANES)).astype(jnp.bfloat16) for h in highs]
                    low = [jnp.broadcast_to(l[feature : feature + 1], (16, LANES)).astype(jnp.bfloat16) for l in lows]
                    for level in range(HIGH):
                        left.append(
                            jnp.concatenate(
                                [jnp.where(h == level, w, zero) for h, w in zip(high, weights)], axis=1
                            )
                        )
                    for level in low_levels:
                        right.append(
                            jnp.concatenate([jnp.where(l <= level, one, zero) for l in low], axis=1)
                        )
                acc[group] += lax.dot_general(
                    jnp.concatenate(left, axis=0),
                    jnp.concatenate(right, axis=0),
                    (((1,), (1,)), ((), ())),
                    preferred_element_type=jnp.float32,
                )
            return carry

        lax.fori_loop(0, blocks // BLOCKS, one_chunk, 0)
        return carry

    lax.fori_loop(0, nr, one_source, 0)

    for feature in range(own):
        group, inner = divmod(feature, GROUP)
        columns = slice(inner * LOW, (inner + 1) * LOW)
        lefts, running = [], [None, None]
        for level in range(HIGH):
            for stat in range(2):
                top = ((inner * HIGH + level) * 2 + stat) * NODES
                part = acc[group, top : top + NODES, columns]
                if level:
                    part = part + running[stat]
                running[stat] = jnp.broadcast_to(part[:, LOW - 1 :], (NODES, LOW))
                lefts.append(part)
        grad_all, hess_all = running
        base = grad_all * grad_all / (hess_all + 1.0)
        for level in range(HIGH):
            grad_left, hess_left = lefts[2 * level], lefts[2 * level + 1]
            rest = grad_all - grad_left
            gain = (
                grad_left * grad_left / (hess_left + 1.0)
                + rest * rest / (hess_all - hess_left + 1.0)
                - base
            )
            turned[level, pl.ds(feature, NODES, stride=own), 0:LOW] = gain

    for level in range(HIGH):
        flipped = jnp.transpose(turned[level])
        for part in range(LOW // slice_bins):
            gain_send[level * (LOW // slice_bins) + part] = flipped[part * slice_bins : (part + 1) * slice_bins]

    def send_gain(step, carry):
        gain_copy(nr - step).start()
        return carry

    lax.fori_loop(1, nr, send_gain, 0)
    gain_recv[my_row] = gain_send[my_row]

    def take_gain(step, carry):
        gain_copy(step).wait_recv()
        return carry

    lax.fori_loop(1, nr, take_gain, 0)
    for source in range(nr):
        for node in range(NODES):
            gain_ref[node, :, source * own : (source + 1) * own] = gain_recv[source, :, node * own : (node + 1) * own]

    def settle(step, carry):
        bin_copy(step).wait_send()
        gain_copy(step).wait_send()
        return carry

    lax.fori_loop(1, nr, settle, 0)
    pltpu.make_async_copy(pay.at[others], pay.at[others], pay_send_sem).wait()
    pltpu.make_async_copy(nodes.at[row_others], nodes.at[row_others], node_send_sem).wait()


def shards(nr, nf, predictor, events, tie_groups, node_ids, bin_index):
    length = predictor.shape[0]
    quarter = length // LANES
    rows = node_ids.shape[0]
    features = bin_index.shape[0]
    own = features // nr
    blocks = rows // LANES
    tile = -(-own // 16) * 16
    groups = -(-own // GROUP)
    all_rows = nr * blocks
    slice_bins = BINS // nr
    vmem = pl.BlockSpec(memory_space=pltpu.VMEM)
    f32, bf16 = jnp.float32, jnp.bfloat16
    gradient, hessian, gain = pl.pallas_call(
        functools.partial(kernel, nr, nf),
        out_shape=(
            jax.ShapeDtypeStruct((quarter, LANES), f32),
            jax.ShapeDtypeStruct((quarter, LANES), f32),
            jax.ShapeDtypeStruct((NODES, slice_bins, features), f32),
        ),
        in_specs=[vmem] * 5,
        out_specs=(vmem,) * 3,
        scratch_shapes=[
            pltpu.VMEM((nr * nf, 2 * quarter, LANES), f32),
            pltpu.VMEM((nr, blocks, LANES), bf16),
            pltpu.VMEM((nr, blocks, tile, LANES), bf16),
            pltpu.VMEM((nr, blocks, tile, LANES), bf16),
            pltpu.VMEM((nr, slice_bins, LANES), f32),
            pltpu.VMEM((nr, slice_bins, LANES), f32),
            pltpu.VMEM((groups, GROUP * HIGH * CHANNELS, GROUP * LOW), f32),
            pltpu.VMEM((HIGH, LANES, LANES), f32),
            pltpu.VMEM((all_rows, LANES), f32),
            pltpu.VMEM((all_rows, LANES), jnp.int32),
            pltpu.VMEM((all_rows, LANES), f32),
            pltpu.VMEM((all_rows, LANES), f32),
            pltpu.VMEM((all_rows, LANES), f32),
            pltpu.SemaphoreType.DMA,
            pltpu.SemaphoreType.DMA,
            pltpu.SemaphoreType.DMA,
            pltpu.SemaphoreType.DMA,
            pltpu.SemaphoreType.DMA((nr,)),
            pltpu.SemaphoreType.DMA((nr,)),
            pltpu.SemaphoreType.DMA((nr,)),
            pltpu.SemaphoreType.DMA((nr,)),
        ],
        compiler_params=pltpu.CompilerParams(
            collective_id=0, has_side_effects=True, vmem_limit_bytes=48 * 1024 * 1024
        ),
    )(
        predictor.reshape(quarter, LANES),
        events.reshape(quarter, LANES),
        tie_groups.reshape(quarter, LANES),
        node_ids.reshape(blocks, LANES),
        bin_index,
    )
    return gradient.reshape(length), hessian.reshape(length), gain.transpose(0, 2, 1)


def solution(mesh):
    return jax.shard_map(
        functools.partial(shards, mesh.shape["row"], mesh.shape["feat"]),
        mesh=mesh,
        in_specs=(
            P(("row", "feat")),
            P(("row", "feat")),
            P(("row", "feat")),
            P("row"),
            P("feat", "row"),
        ),
        out_specs=(P(("row", "feat")), P(("row", "feat")), P(None, "feat", "row")),
        check_vma=False,
    )
```

```python
import functools

import jax
import jax.numpy as jnp
from jax import lax
from jax.experimental import pallas as pl
from jax.experimental.pallas import tpu as pltpu
from jax.sharding import PartitionSpec as P

BINS = 256
NODES = 8
LANES = 128
HIGH = 4
LOW = BINS // HIGH
CHANNELS = 2 * NODES
GROUP = 2
BLOCKS = 4
MESH = pl.DeviceIdType.MESH
EXACT = lax.Precision.HIGHEST


def partner(me, step, count):
    other = me
    bit = 1
    while bit < count:
        other = other + ((step // bit) % 2) * bit * (1 - 2 * ((me // bit) % 2))
        bit *= 2
    return other


def triangle(rows, columns, keep):
    a = lax.broadcasted_iota(jnp.int32, (rows, columns), 0)
    b = lax.broadcasted_iota(jnp.int32, (rows, columns), 1)
    return keep(a, b).astype(jnp.float32)


def exact_dot(a, b):
    return jnp.dot(a, b, precision=EXACT, preferred_element_type=jnp.float32)


def fill(value, known, step):
    for distance in (1, 2, 4):
        shift = distance if step > 0 else LANES - distance
        value = jnp.where(known > 0, value, pltpu.roll(value, shift, 1))
        known = jnp.maximum(known, pltpu.roll(known, shift, 1))
    return value


def cox(score, code):
    rows = score.shape[0]
    hazard_exp = jnp.exp(score)
    tie = code // 2
    failed = (code - 2 * tie).astype(jnp.float32)
    lane = lax.broadcasted_iota(jnp.int32, (rows, LANES), 1)
    begins = ((lane % 8 == 0) | (tie != pltpu.roll(tie, 1, 1))).astype(jnp.float32)
    finish = pltpu.roll(begins, LANES - 1, 1)
    lane_suffix = exact_dot(hazard_exp, triangle(LANES, LANES, lambda a, b: a >= b))
    whole = jnp.broadcast_to(lane_suffix[:, :1], (rows, LANES))
    suffix = lane_suffix + exact_dot(triangle(rows, rows, lambda a, b: b > a), whole)
    risk_sum = fill(suffix, begins, 1)
    weight_one = failed / risk_sum
    weight_two = failed / (risk_sum * risk_sum)
    upper = triangle(LANES, LANES, lambda a, b: a <= b)
    earlier = triangle(rows, rows, lambda a, b: b < a)

    def running(weight):
        within = exact_dot(weight, upper)
        whole = jnp.broadcast_to(within[:, LANES - 1 :], (rows, LANES))
        return fill(within + exact_dot(earlier, whole), finish, -1)

    hazard_one = running(weight_one)
    hazard_two = running(weight_two)
    gradient = hazard_exp * hazard_one - failed
    hessian = hazard_exp * hazard_one - hazard_exp * hazard_exp * hazard_two
    return gradient, hessian


def kernel(
    nr, nf, pred_hbm, event_hbm, tie_hbm, node_hbm, bin_hbm, grad_ref, hess_ref, gain_ref,
    pred_ref, event_ref, tie_ref, node_ref, bin_ref, highs, lows, weights,
    pay, nodes, bin_send, bin_recv, gain_send, gain_recv, acc, turned, score, code, grads, hesss,
    levelled, in_sem, pay_send_sem, pay_sem, node_send_sem, node_sem, bin_send_sem, bin_sem, gain_send_sem, gain_sem,
):
    my_row = lax.axis_index("row")
    my_feat = lax.axis_index("feat")
    me = my_row * nf + my_feat
    count = nr * nf
    quarter = pred_ref.shape[0]
    blocks = bin_ref.shape[1] // LANES
    own = bin_ref.shape[0] // nr
    tile = bin_send.shape[2]
    slice_bins = BINS // nr

    def coords(device):
        return (device // nf, device % nf)

    reads = [
        pltpu.make_async_copy(source, target, in_sem.at[place])
        for place, (source, target) in enumerate(
            [(pred_hbm, pred_ref), (event_hbm, event_ref), (tie_hbm, tie_ref), (node_hbm, node_ref), (bin_hbm, bin_ref)]
        )
    ]
    for read in reads:
        read.start()
    barrier = pltpu.get_barrier_semaphore()

    def greet(step, carry):
        other = (me + step) % count
        pl.semaphore_signal(barrier, inc=1, device_id=coords(other), device_id_type=MESH)
        return carry

    lax.fori_loop(1, count, greet, 0)

    for read in reads[:4]:
        read.wait()
    pay[me, 0:quarter, :] = pred_ref[...]
    pay[me, quarter : 2 * quarter, :] = (tie_ref[...] * 2 + event_ref[...]).astype(jnp.float32)
    nodes[my_row] = node_ref[...].astype(jnp.float32).astype(jnp.bfloat16)

    reads[4].wait()

    def pack(block, carry):
        lanes = pl.ds(pl.multiple_of(block * LANES, LANES), LANES)
        for target in range(nr):
            part = bin_ref[target * own : (target + 1) * own, lanes].astype(jnp.float32)
            if own < tile:
                part = jnp.concatenate([part, jnp.zeros((tile - own, LANES), jnp.float32)], axis=0)
            bin_send[target, block] = part.astype(jnp.bfloat16)
        return carry

    lax.fori_loop(0, blocks, pack, 0)
    pl.semaphore_wait(barrier, count - 1)

    def pay_copy(other):
        return pltpu.make_async_remote_copy(
            src_ref=pay.at[me], dst_ref=pay.at[me], send_sem=pay_send_sem, recv_sem=pay_sem,
            device_id=coords(other), device_id_type=MESH,
        )

    def node_copy(step):
        other = partner(my_row, step, nr)
        return pltpu.make_async_remote_copy(
            src_ref=nodes.at[my_row], dst_ref=nodes.at[my_row],
            send_sem=node_send_sem, recv_sem=node_sem,
            device_id=(other, my_feat), device_id_type=MESH,
        )

    def bin_copy(step):
        other = partner(my_row, step, nr)
        return pltpu.make_async_remote_copy(
            src_ref=bin_send.at[other], dst_ref=bin_recv.at[my_row],
            send_sem=bin_send_sem.at[step], recv_sem=bin_sem.at[step],
            device_id=(other, my_feat), device_id_type=MESH,
        )

    def gain_copy(step):
        other = partner(my_row, step, nr)
        return pltpu.make_async_remote_copy(
            src_ref=gain_send.at[other], dst_ref=gain_recv.at[my_row],
            send_sem=gain_send_sem.at[step], recv_sem=gain_sem.at[step],
            device_id=(other, my_feat), device_id_type=MESH,
        )

    def send_pay(step, carry):
        pay_copy((me + step) % count).start()
        return carry

    lax.fori_loop(1, count, send_pay, 0)

    def send_nodes(step, carry):
        node_copy(step).start()
        return carry

    lax.fori_loop(1, nr, send_nodes, 0)

    def send_bins(step, carry):
        bin_copy(nr - step).start()
        return carry

    lax.fori_loop(1, nr, send_bins, 0)

    bin_recv[my_row] = bin_send[my_row]
    acc[...] = jnp.zeros_like(acc)

    others = pl.ds(0, count - 1)
    pltpu.make_async_copy(pay.at[others], pay.at[others], pay_sem).wait()

    def spread(device, carry):
        rows = pl.ds(device * quarter, quarter)
        score[rows, :] = pay[device, 0:quarter, :]
        code[rows, :] = pay[device, quarter : 2 * quarter, :].astype(jnp.int32)
        return carry

    lax.fori_loop(0, count, spread, 0)
    gradient, hessian = cox(score[...], code[...])
    grads[...] = gradient
    hesss[...] = hessian
    mine = pl.ds(me * quarter, quarter)
    grad_ref[...] = grads[mine, :]
    hess_ref[...] = hesss[mine, :]

    row_others = pl.ds(0, nr - 1)
    pltpu.make_async_copy(nodes.at[row_others], nodes.at[row_others], node_sem).wait()
    for source in range(nr):
        levelled[source * blocks : (source + 1) * blocks, :] = nodes[source].astype(jnp.float32)

    levels = lax.broadcasted_iota(jnp.int32, (NODES, LANES), 0).astype(jnp.float32)
    low_levels = [
        (lax.broadcasted_iota(jnp.int32, (16, LANES), 0) + 16 * part).astype(jnp.float32).astype(jnp.bfloat16)
        for part in range(LOW // 16)
    ]
    one = jnp.ones((16, LANES), jnp.bfloat16)
    zero = jnp.zeros((16, LANES), jnp.bfloat16)
    groups = -(-own // GROUP)

    def one_source(step, carry):
        source = partner(my_row, step, nr)

        @pl.when(step > 0)
        def _():
            bin_copy(step).wait_recv()

        for block in range(blocks):
            row = pl.ds(source * blocks + block, 1)
            is_node = jnp.broadcast_to(levelled[row, :], (NODES, LANES)) == levels
            weight = jnp.concatenate(
                [
                    jnp.where(is_node, jnp.broadcast_to(grads[row, :], (NODES, LANES)), 0.0),
                    jnp.where(is_node, jnp.broadcast_to(hesss[row, :], (NODES, LANES)), 0.0),
                ],
                axis=0,
            )
            weights[block] = weight.astype(jnp.bfloat16)
            bins = bin_recv[source, block].astype(jnp.float32)
            high = jnp.floor(bins * (1.0 / LOW))
            highs[block] = high
            lows[block] = bins - high * LOW

        def one_chunk(chunk, carry):
            here = [chunk * BLOCKS + inner for inner in range(BLOCKS)]
            weight = [weights[block] for block in here]

            def row_of(ref, block, feature):
                row = ref[block, feature : feature + 1, :]
                return jnp.broadcast_to(row, (16, LANES)).astype(jnp.bfloat16)

            for group in range(groups):
                left, right = [], []
                for inner in range(GROUP):
                    feature = group * GROUP + inner
                    high = [row_of(highs, block, feature) for block in here]
                    low = [row_of(lows, block, feature) for block in here]
                    for level in range(HIGH):
                        left.append(
                            jnp.concatenate(
                                [jnp.where(h == level, w, zero) for h, w in zip(high, weight)], axis=1
                            )
                        )
                    for level in low_levels:
                        right.append(
                            jnp.concatenate([jnp.where(l <= level, one, zero) for l in low], axis=1)
                        )
                acc[group] += lax.dot_general(
                    jnp.concatenate(left, axis=0),
                    jnp.concatenate(right, axis=0),
                    (((1,), (1,)), ((), ())),
                    preferred_element_type=jnp.float32,
                )
            return carry

        lax.fori_loop(0, blocks // BLOCKS, one_chunk, 0)
        return carry

    lax.fori_loop(0, nr, one_source, 0)

    for feature in range(own):
        group, inner = divmod(feature, GROUP)
        columns = slice(inner * LOW, (inner + 1) * LOW)
        lefts, running = [], [None, None]
        for level in range(HIGH):
            for stat in range(2):
                top = ((inner * HIGH + level) * 2 + stat) * NODES
                part = acc[group, top : top + NODES, columns]
                if level:
                    part = part + running[stat]
                running[stat] = jnp.broadcast_to(part[:, LOW - 1 :], (NODES, LOW))
                lefts.append(part)
        grad_all, hess_all = running
        base = grad_all * grad_all / (hess_all + 1.0)
        for level in range(HIGH):
            grad_left, hess_left = lefts[2 * level], lefts[2 * level + 1]
            rest = grad_all - grad_left
            gain = (
                grad_left * grad_left / (hess_left + 1.0)
                + rest * rest / (hess_all - hess_left + 1.0)
                - base
            )
            turned[level, pl.ds(feature, NODES, stride=own), 0:LOW] = gain

    for level in range(HIGH):
        flipped = jnp.transpose(turned[level])
        for part in range(LOW // slice_bins):
            gain_send[level * (LOW // slice_bins) + part] = flipped[part * slice_bins : (part + 1) * slice_bins]

    def send_gain(step, carry):
        gain_copy(nr - step).start()
        return carry

    lax.fori_loop(1, nr, send_gain, 0)
    gain_recv[my_row] = gain_send[my_row]

    def take_gain(step, carry):
        gain_copy(step).wait_recv()
        return carry

    lax.fori_loop(1, nr, take_gain, 0)
    for source in range(nr):
        for node in range(NODES):
            gain_ref[node, :, source * own : (source + 1) * own] = gain_recv[source, :, node * own : (node + 1) * own]

    def settle(step, carry):
        bin_copy(step).wait_send()
        gain_copy(step).wait_send()
        return carry

    lax.fori_loop(1, nr, settle, 0)
    pltpu.make_async_copy(pay.at[others], pay.at[others], pay_send_sem).wait()
    pltpu.make_async_copy(nodes.at[row_others], nodes.at[row_others], node_send_sem).wait()


def shards(nr, nf, predictor, events, tie_groups, node_ids, bin_index):
    length = predictor.shape[0]
    quarter = length // LANES
    rows = node_ids.shape[0]
    features = bin_index.shape[0]
    own = features // nr
    blocks = rows // LANES
    tile = -(-own // 16) * 16
    groups = -(-own // GROUP)
    all_rows = nr * blocks
    slice_bins = BINS // nr
    vmem = pl.BlockSpec(memory_space=pltpu.VMEM)
    f32, bf16 = jnp.float32, jnp.bfloat16
    gradient, hessian, gain = pl.pallas_call(
        functools.partial(kernel, nr, nf),
        out_shape=(
            jax.ShapeDtypeStruct((quarter, LANES), f32),
            jax.ShapeDtypeStruct((quarter, LANES), f32),
            jax.ShapeDtypeStruct((NODES, slice_bins, features), f32),
        ),
        in_specs=[pl.BlockSpec(memory_space=pltpu.HBM)] * 5,
        out_specs=(vmem,) * 3,
        scratch_shapes=[
            pltpu.VMEM((quarter, LANES), f32),
            pltpu.VMEM((quarter, LANES), jnp.int32),
            pltpu.VMEM((quarter, LANES), jnp.int32),
            pltpu.VMEM((blocks, LANES), jnp.int32),
            pltpu.VMEM((features, rows), jnp.int32),
            pltpu.VMEM((blocks, tile, LANES), f32),
            pltpu.VMEM((blocks, tile, LANES), f32),
            pltpu.VMEM((blocks, CHANNELS, LANES), bf16),
            pltpu.VMEM((nr * nf, 2 * quarter, LANES), f32),
            pltpu.VMEM((nr, blocks, LANES), bf16),
            pltpu.VMEM((nr, blocks, tile, LANES), bf16),
            pltpu.VMEM((nr, blocks, tile, LANES), bf16),
            pltpu.VMEM((nr, slice_bins, LANES), f32),
            pltpu.VMEM((nr, slice_bins, LANES), f32),
            pltpu.VMEM((groups, GROUP * HIGH * CHANNELS, GROUP * LOW), f32),
            pltpu.VMEM((HIGH, LANES, LANES), f32),
            pltpu.VMEM((all_rows, LANES), f32),
            pltpu.VMEM((all_rows, LANES), jnp.int32),
            pltpu.VMEM((all_rows, LANES), f32),
            pltpu.VMEM((all_rows, LANES), f32),
            pltpu.VMEM((all_rows, LANES), f32),
            pltpu.SemaphoreType.DMA((5,)),
            pltpu.SemaphoreType.DMA,
            pltpu.SemaphoreType.DMA,
            pltpu.SemaphoreType.DMA,
            pltpu.SemaphoreType.DMA,
            pltpu.SemaphoreType.DMA((nr,)),
            pltpu.SemaphoreType.DMA((nr,)),
            pltpu.SemaphoreType.DMA((nr,)),
            pltpu.SemaphoreType.DMA((nr,)),
        ],
        compiler_params=pltpu.CompilerParams(
            collective_id=0, has_side_effects=True, vmem_limit_bytes=63 * 1024 * 1024
        ),
    )(
        predictor.reshape(quarter, LANES),
        events.reshape(quarter, LANES),
        tie_groups.reshape(quarter, LANES),
        node_ids.reshape(blocks, LANES),
        bin_index,
    )
    return gradient.reshape(length), hessian.reshape(length), gain.transpose(0, 2, 1)


def solution(mesh):
    return jax.shard_map(
        functools.partial(shards, mesh.shape["row"], mesh.shape["feat"]),
        mesh=mesh,
        in_specs=(
            P(("row", "feat")),
            P(("row", "feat")),
            P(("row", "feat")),
            P("row"),
            P("feat", "row"),
        ),
        out_specs=(P(("row", "feat")), P(("row", "feat")), P(None, "feat", "row")),
        check_vma=False,
    )
```

```python
import functools

import jax
import jax.numpy as jnp
from jax import lax
from jax.experimental import pallas as pl
from jax.experimental.pallas import tpu as pltpu
from jax.sharding import PartitionSpec as P

BINS = 256
NODES = 8
LANES = 128
HIGH = 4
LOW = BINS // HIGH
CHANNELS = 2 * NODES
GROUP = 2
BLOCKS = 4
MESH = pl.DeviceIdType.MESH
EXACT = lax.Precision.HIGHEST


def partner(me, step, count):
    other = me
    bit = 1
    while bit < count:
        other = other + ((step // bit) % 2) * bit * (1 - 2 * ((me // bit) % 2))
        bit *= 2
    return other


def step_of(place, count):
    half = count // 2
    odd = place % 2
    last = place // (count - 1)
    later = (place + count - 1) // count
    by_turns = odd * ((place + 1) // 2) + (1 - odd) * later * (half + place // 2 - 1)
    return (1 - last) * by_turns + last * (count - 1)


def triangle(rows, columns, keep):
    a = lax.broadcasted_iota(jnp.int32, (rows, columns), 0)
    b = lax.broadcasted_iota(jnp.int32, (rows, columns), 1)
    return keep(a, b).astype(jnp.float32)


def exact_dot(a, b):
    return jnp.dot(a, b, precision=EXACT, preferred_element_type=jnp.float32)


def fill(value, known, step):
    for distance in (1, 2, 4):
        shift = distance if step > 0 else LANES - distance
        value = jnp.where(known > 0, value, pltpu.roll(value, shift, 1))
        known = jnp.maximum(known, pltpu.roll(known, shift, 1))
    return value


def cox(score, code):
    rows = score.shape[0]
    hazard_exp = jnp.exp(score)
    tie = code // 2
    failed = (code - 2 * tie).astype(jnp.float32)
    lane = lax.broadcasted_iota(jnp.int32, (rows, LANES), 1)
    begins = ((lane % 8 == 0) | (tie != pltpu.roll(tie, 1, 1))).astype(jnp.float32)
    finish = pltpu.roll(begins, LANES - 1, 1)
    lane_suffix = exact_dot(hazard_exp, triangle(LANES, LANES, lambda a, b: a >= b))
    whole = jnp.broadcast_to(lane_suffix[:, :1], (rows, LANES))
    suffix = lane_suffix + exact_dot(triangle(rows, rows, lambda a, b: b > a), whole)
    risk_sum = fill(suffix, begins, 1)
    weight_one = failed / risk_sum
    weight_two = failed / (risk_sum * risk_sum)
    upper = triangle(LANES, LANES, lambda a, b: a <= b)
    earlier = triangle(rows, rows, lambda a, b: b < a)

    def running(weight):
        within = exact_dot(weight, upper)
        whole = jnp.broadcast_to(within[:, LANES - 1 :], (rows, LANES))
        return fill(within + exact_dot(earlier, whole), finish, -1)

    hazard_one = running(weight_one)
    hazard_two = running(weight_two)
    gradient = hazard_exp * hazard_one - failed
    hessian = hazard_exp * hazard_one - hazard_exp * hazard_exp * hazard_two
    return gradient, hessian


def kernel(
    nr, nf, pred_hbm, event_hbm, tie_hbm, node_hbm, bin_hbm, grad_ref, hess_ref, gain_ref,
    pred_ref, event_ref, tie_ref, node_ref, bin_ref, highs, lows, weights,
    pay, bin_send, bin_recv, gain_send, gain_recv, acc, turned, score, code, grads, hesss,
    levelled, in_sem, row_send_sem, row_sem, feat_send_sem, feat_sem, bin_send_sem, bin_sem, gain_send_sem, gain_sem,
):
    my_row = lax.axis_index("row")
    my_feat = lax.axis_index("feat")
    me = my_row * nf + my_feat
    quarter = pred_ref.shape[0]
    blocks = bin_ref.shape[1] // LANES
    own = bin_ref.shape[0] // nr
    tile = bin_send.shape[2]
    slice_bins = BINS // nr

    reads = [
        pltpu.make_async_copy(source, target, in_sem.at[place])
        for place, (source, target) in enumerate(
            [(pred_hbm, pred_ref), (event_hbm, event_ref), (tie_hbm, tie_ref), (node_hbm, node_ref), (bin_hbm, bin_ref)]
        )
    ]
    for read in reads:
        read.start()
    barrier = pltpu.get_barrier_semaphore()

    def greet_row(step, carry):
        other = (my_row + step) % nr
        pl.semaphore_signal(barrier, inc=1, device_id=(other, my_feat), device_id_type=MESH)
        return carry

    def greet_feat(step, carry):
        other = (my_feat + step) % nf
        pl.semaphore_signal(barrier, inc=1, device_id=(my_row, other), device_id_type=MESH)
        return carry

    lax.fori_loop(1, nr, greet_row, 0)
    lax.fori_loop(1, nf, greet_feat, 0)

    for read in reads[:4]:
        read.wait()
    pay[my_feat, my_row, 0:quarter, :] = pred_ref[...]
    pay[my_feat, my_row, quarter : 2 * quarter, :] = (tie_ref[...] * 2 + event_ref[...]).astype(jnp.float32)
    share = node_ref[pl.ds(my_feat * quarter, quarter), :]
    pay[my_feat, my_row, 2 * quarter : 3 * quarter, :] = share.astype(jnp.float32)
    reads[4].wait()

    def pack(block, carry):
        lanes = pl.ds(pl.multiple_of(block * LANES, LANES), LANES)
        for target in range(nr):
            part = bin_ref[target * own : (target + 1) * own, lanes].astype(jnp.float32)
            if own < tile:
                part = jnp.concatenate([part, jnp.zeros((tile - own, LANES), jnp.float32)], axis=0)
            bin_send[target, block] = part.astype(jnp.bfloat16)
        return carry

    lax.fori_loop(0, blocks, pack, 0)
    pl.semaphore_wait(barrier, nr + nf - 2)

    def row_copy(step):
        other = partner(my_row, step, nr)
        mine = pay.at[my_feat, my_row]
        return pltpu.make_async_remote_copy(
            src_ref=mine, dst_ref=mine, send_sem=row_send_sem, recv_sem=row_sem,
            device_id=(other, my_feat), device_id_type=MESH,
        )

    def feat_copy(step):
        other = (my_feat + step) % nf
        return pltpu.make_async_remote_copy(
            src_ref=pay.at[my_feat], dst_ref=pay.at[my_feat],
            send_sem=feat_send_sem, recv_sem=feat_sem,
            device_id=(my_row, other), device_id_type=MESH,
        )

    def bin_copy(step):
        other = partner(my_row, step, nr)
        return pltpu.make_async_remote_copy(
            src_ref=bin_send.at[other], dst_ref=bin_recv.at[my_row],
            send_sem=bin_send_sem.at[step], recv_sem=bin_sem.at[step],
            device_id=(other, my_feat), device_id_type=MESH,
        )

    def gain_copy(step):
        other = partner(my_row, step, nr)
        return pltpu.make_async_remote_copy(
            src_ref=gain_send.at[other], dst_ref=gain_recv.at[my_row],
            send_sem=gain_send_sem.at[step], recv_sem=gain_sem.at[step],
            device_id=(other, my_feat), device_id_type=MESH,
        )

    def send_row(step, carry):
        row_copy(nr - step).start()
        return carry

    lax.fori_loop(1, nr, send_row, 0)

    def send_bins(place, carry):
        bin_copy(step_of(place, nr)).start()
        return carry

    lax.fori_loop(1, nr, send_bins, 0)

    bin_recv[my_row] = bin_send[my_row]
    acc[...] = jnp.zeros_like(acc)

    row_bytes = pay.at[0, pl.ds(0, nr - 1)]
    feat_bytes = pay.at[pl.ds(0, nf - 1)]
    pltpu.make_async_copy(row_bytes, row_bytes, row_sem).wait()

    def send_feat(step, carry):
        feat_copy(step).start()
        return carry

    lax.fori_loop(1, nf, send_feat, 0)
    pltpu.make_async_copy(feat_bytes, feat_bytes, feat_sem).wait()

    def spread(row, carry):
        for feat in range(nf):
            rows = pl.ds((row * nf + feat) * quarter, quarter)
            score[rows, :] = pay[feat, row, 0:quarter, :]
            code[rows, :] = pay[feat, row, quarter : 2 * quarter, :].astype(jnp.int32)
            levelled[rows, :] = pay[feat, row, 2 * quarter : 3 * quarter, :]
        return carry

    lax.fori_loop(0, nr, spread, 0)
    gradient, hessian = cox(score[...], code[...])
    grads[...] = gradient
    hesss[...] = hessian
    mine = pl.ds(me * quarter, quarter)
    grad_ref[...] = grads[mine, :]
    hess_ref[...] = hesss[mine, :]

    levels = lax.broadcasted_iota(jnp.int32, (NODES, LANES), 0).astype(jnp.float32)
    low_levels = [
        (lax.broadcasted_iota(jnp.int32, (16, LANES), 0) + 16 * part).astype(jnp.float32).astype(jnp.bfloat16)
        for part in range(LOW // 16)
    ]
    one = jnp.ones((16, LANES), jnp.bfloat16)
    zero = jnp.zeros((16, LANES), jnp.bfloat16)
    groups = -(-own // GROUP)

    def one_source(place, carry):
        step = step_of(place, nr)
        source = partner(my_row, step, nr)

        @pl.when(place > 0)
        def _():
            bin_copy(step).wait_recv()

        for block in range(blocks):
            row = pl.ds(source * blocks + block, 1)
            is_node = jnp.broadcast_to(levelled[row, :], (NODES, LANES)) == levels
            weight = jnp.concatenate(
                [
                    jnp.where(is_node, jnp.broadcast_to(grads[row, :], (NODES, LANES)), 0.0),
                    jnp.where(is_node, jnp.broadcast_to(hesss[row, :], (NODES, LANES)), 0.0),
                ],
                axis=0,
            )
            weights[block] = weight.astype(jnp.bfloat16)
            bins = bin_recv[source, block].astype(jnp.float32)
            high = jnp.floor(bins * (1.0 / LOW))
            highs[block] = high
            lows[block] = bins - high * LOW

        def one_chunk(chunk, carry):
            here = [chunk * BLOCKS + inner for inner in range(BLOCKS)]
            weight = [weights[block] for block in here]

            def row_of(ref, block, feature):
                row = ref[block, feature : feature + 1, :]
                return jnp.broadcast_to(row, (16, LANES)).astype(jnp.bfloat16)

            for group in range(groups):
                left, right = [], []
                for inner in range(GROUP):
                    feature = group * GROUP + inner
                    high = [row_of(highs, block, feature) for block in here]
                    low = [row_of(lows, block, feature) for block in here]
                    for level in range(HIGH - 1):
                        left.append(
                            jnp.concatenate(
                                [jnp.where(h <= level, w, zero) for h, w in zip(high, weight)], axis=1
                            )
                        )
                    left.append(jnp.concatenate(weight, axis=1))
                    for level in low_levels:
                        right.append(
                            jnp.concatenate([jnp.where(l <= level, one, zero) for l in low], axis=1)
                        )
                acc[group] += lax.dot_general(
                    jnp.concatenate(left, axis=0),
                    jnp.concatenate(right, axis=0),
                    (((1,), (1,)), ((), ())),
                    preferred_element_type=jnp.float32,
                )
            return carry

        lax.fori_loop(0, blocks // BLOCKS, one_chunk, 0)
        return carry

    lax.fori_loop(0, nr, one_source, 0)

    for feature in range(own):
        group, inner = divmod(feature, GROUP)
        columns = slice(inner * LOW, (inner + 1) * LOW)
        lefts, before, running = [], [None, None], [None, None]
        for level in range(HIGH):
            for stat in range(2):
                top = ((inner * HIGH + level) * 2 + stat) * NODES
                part = acc[group, top : top + NODES, columns]
                lefts.append(running[stat] + (part - before[stat]) if level else part)
                before[stat] = part
                running[stat] = jnp.broadcast_to(part[:, LOW - 1 :], (NODES, LOW))
        grad_all, hess_all = running
        base = grad_all * grad_all / (hess_all + 1.0)
        for level in range(HIGH):
            grad_left, hess_left = lefts[2 * level], lefts[2 * level + 1]
            rest = grad_all - grad_left
            gain = (
                grad_left * grad_left / (hess_left + 1.0)
                + rest * rest / (hess_all - hess_left + 1.0)
                - base
            )
            turned[level, pl.ds(feature, NODES, stride=own), 0:LOW] = gain

    for level in range(HIGH):
        flipped = jnp.transpose(turned[level])
        for part in range(LOW // slice_bins):
            gain_send[level * (LOW // slice_bins) + part] = flipped[part * slice_bins : (part + 1) * slice_bins]

    def send_gain(step, carry):
        gain_copy(nr - step).start()
        return carry

    lax.fori_loop(1, nr, send_gain, 0)
    gain_recv[my_row] = gain_send[my_row]

    def take_gain(step, carry):
        gain_copy(step).wait_recv()
        return carry

    lax.fori_loop(1, nr, take_gain, 0)
    for source in range(nr):
        for node in range(NODES):
            gain_ref[node, :, source * own : (source + 1) * own] = gain_recv[source, :, node * own : (node + 1) * own]

    def settle(step, carry):
        bin_copy(step).wait_send()
        gain_copy(step).wait_send()
        return carry

    lax.fori_loop(1, nr, settle, 0)
    pltpu.make_async_copy(row_bytes, row_bytes, row_send_sem).wait()
    pltpu.make_async_copy(feat_bytes, feat_bytes, feat_send_sem).wait()


def shards(nr, nf, predictor, events, tie_groups, node_ids, bin_index):
    length = predictor.shape[0]
    quarter = length // LANES
    rows = node_ids.shape[0]
    features = bin_index.shape[0]
    own = features // nr
    blocks = rows // LANES
    tile = -(-own // 16) * 16
    groups = -(-own // GROUP)
    all_rows = nr * blocks
    slice_bins = BINS // nr
    vmem = pl.BlockSpec(memory_space=pltpu.VMEM)
    f32, bf16 = jnp.float32, jnp.bfloat16
    gradient, hessian, gain = pl.pallas_call(
        functools.partial(kernel, nr, nf),
        out_shape=(
            jax.ShapeDtypeStruct((quarter, LANES), f32),
            jax.ShapeDtypeStruct((quarter, LANES), f32),
            jax.ShapeDtypeStruct((NODES, slice_bins, features), f32),
        ),
        in_specs=[pl.BlockSpec(memory_space=pltpu.HBM)] * 5,
        out_specs=(vmem,) * 3,
        scratch_shapes=[
            pltpu.VMEM((quarter, LANES), f32),
            pltpu.VMEM((quarter, LANES), jnp.int32),
            pltpu.VMEM((quarter, LANES), jnp.int32),
            pltpu.VMEM((blocks, LANES), jnp.int32),
            pltpu.VMEM((features, rows), jnp.int32),
            pltpu.VMEM((blocks, tile, LANES), f32),
            pltpu.VMEM((blocks, tile, LANES), f32),
            pltpu.VMEM((blocks, CHANNELS, LANES), bf16),
            pltpu.VMEM((nf, nr, -(-3 * quarter // 8) * 8, LANES), f32),
            pltpu.VMEM((nr, blocks, tile, LANES), bf16),
            pltpu.VMEM((nr, blocks, tile, LANES), bf16),
            pltpu.VMEM((nr, slice_bins, LANES), f32),
            pltpu.VMEM((nr, slice_bins, LANES), f32),
            pltpu.VMEM((groups, GROUP * HIGH * CHANNELS, GROUP * LOW), f32),
            pltpu.VMEM((HIGH, LANES, LANES), f32),
            pltpu.VMEM((all_rows, LANES), f32),
            pltpu.VMEM((all_rows, LANES), jnp.int32),
            pltpu.VMEM((all_rows, LANES), f32),
            pltpu.VMEM((all_rows, LANES), f32),
            pltpu.VMEM((all_rows, LANES), f32),
            pltpu.SemaphoreType.DMA((5,)),
            pltpu.SemaphoreType.DMA,
            pltpu.SemaphoreType.DMA,
            pltpu.SemaphoreType.DMA,
            pltpu.SemaphoreType.DMA,
            pltpu.SemaphoreType.DMA((nr,)),
            pltpu.SemaphoreType.DMA((nr,)),
            pltpu.SemaphoreType.DMA((nr,)),
            pltpu.SemaphoreType.DMA((nr,)),
        ],
        compiler_params=pltpu.CompilerParams(
            collective_id=0, has_side_effects=True, vmem_limit_bytes=63 * 1024 * 1024
        ),
    )(
        predictor.reshape(quarter, LANES),
        events.reshape(quarter, LANES),
        tie_groups.reshape(quarter, LANES),
        node_ids.reshape(blocks, LANES),
        bin_index,
    )
    return gradient.reshape(length), hessian.reshape(length), gain.transpose(0, 2, 1)


def solution(mesh):
    return jax.shard_map(
        functools.partial(shards, mesh.shape["row"], mesh.shape["feat"]),
        mesh=mesh,
        in_specs=(
            P(("row", "feat")),
            P(("row", "feat")),
            P(("row", "feat")),
            P("row"),
            P("feat", "row"),
        ),
        out_specs=(P(("row", "feat")), P(("row", "feat")), P(None, "feat", "row")),
        check_vma=False,
    )
```

```python
import functools

import jax
import jax.numpy as jnp
from jax import lax
from jax.experimental import pallas as pl
from jax.experimental.pallas import tpu as pltpu
from jax.sharding import PartitionSpec as P

BINS = 256
NODES = 8
LANES = 128
HIGH = 4
LOW = BINS // HIGH
CHANNELS = 2 * NODES
GROUP = 2
BLOCKS = 8
MESH = pl.DeviceIdType.MESH
EXACT = lax.Precision.HIGHEST


def partner(me, step, count):
    other = me
    bit = 1
    while bit < count:
        other = other + ((step // bit) % 2) * bit * (1 - 2 * ((me // bit) % 2))
        bit *= 2
    return other


def step_of(place, count):
    half = count // 2
    odd = place % 2
    last = place // (count - 1)
    later = (place + count - 1) // count
    by_turns = odd * ((place + 1) // 2) + (1 - odd) * later * (half + place // 2 - 1)
    return (1 - last) * by_turns + last * (count - 1)


def triangle(rows, columns, keep):
    a = lax.broadcasted_iota(jnp.int32, (rows, columns), 0)
    b = lax.broadcasted_iota(jnp.int32, (rows, columns), 1)
    return keep(a, b).astype(jnp.float32)


def exact_dot(a, b):
    return jnp.dot(a, b, precision=EXACT, preferred_element_type=jnp.float32)


def fill(value, known, step):
    for distance in (1, 2, 4):
        shift = distance if step > 0 else LANES - distance
        value = jnp.where(known > 0, value, pltpu.roll(value, shift, 1))
        known = jnp.maximum(known, pltpu.roll(known, shift, 1))
    return value


def cox(score, code):
    rows = score.shape[0]
    hazard_exp = jnp.exp(score)
    tie = code // 2
    failed = (code - 2 * tie).astype(jnp.float32)
    lane = lax.broadcasted_iota(jnp.int32, (rows, LANES), 1)
    begins = ((lane % 8 == 0) | (tie != pltpu.roll(tie, 1, 1))).astype(jnp.float32)
    finish = pltpu.roll(begins, LANES - 1, 1)
    lane_suffix = exact_dot(hazard_exp, triangle(LANES, LANES, lambda a, b: a >= b))
    whole = jnp.broadcast_to(lane_suffix[:, :1], (rows, LANES))
    suffix = lane_suffix + exact_dot(triangle(rows, rows, lambda a, b: b > a), whole)
    risk_sum = fill(suffix, begins, 1)
    weight_one = failed / risk_sum
    weight_two = failed / (risk_sum * risk_sum)
    upper = triangle(LANES, LANES, lambda a, b: a <= b)
    earlier = triangle(rows, rows, lambda a, b: b < a)

    def running(weight):
        within = exact_dot(weight, upper)
        whole = jnp.broadcast_to(within[:, LANES - 1 :], (rows, LANES))
        return fill(within + exact_dot(earlier, whole), finish, -1)

    hazard_one = running(weight_one)
    hazard_two = running(weight_two)
    gradient = hazard_exp * hazard_one - failed
    hessian = hazard_exp * hazard_one - hazard_exp * hazard_exp * hazard_two
    return gradient, hessian


def kernel(
    nr, nf, pred_hbm, event_hbm, tie_hbm, node_hbm, bin_hbm, grad_ref, hess_ref, gain_ref,
    pred_ref, event_ref, tie_ref, node_ref, bin_ref, highs, lows, weights,
    pay, bin_send, bin_recv, gain_send, gain_recv, acc, turned, score, code, grads, hesss,
    levelled, in_sem, row_send_sem, row_sem, feat_send_sem, feat_sem, bin_send_sem, bin_sem, gain_send_sem, gain_sem,
):
    my_row = lax.axis_index("row")
    my_feat = lax.axis_index("feat")
    me = my_row * nf + my_feat
    quarter = pred_ref.shape[0]
    blocks = bin_ref.shape[1] // LANES
    own = bin_ref.shape[0] // nr
    tile = bin_send.shape[2]
    slice_bins = BINS // nr

    reads = [
        pltpu.make_async_copy(source, target, in_sem.at[place])
        for place, (source, target) in enumerate(
            [(pred_hbm, pred_ref), (event_hbm, event_ref), (tie_hbm, tie_ref), (node_hbm, node_ref), (bin_hbm, bin_ref)]
        )
    ]
    for read in reads:
        read.start()
    barrier = pltpu.get_barrier_semaphore()

    def greet_row(step, carry):
        other = (my_row + step) % nr
        pl.semaphore_signal(barrier, inc=1, device_id=(other, my_feat), device_id_type=MESH)
        return carry

    def greet_feat(step, carry):
        other = (my_feat + step) % nf
        pl.semaphore_signal(barrier, inc=1, device_id=(my_row, other), device_id_type=MESH)
        return carry

    lax.fori_loop(1, nr, greet_row, 0)
    lax.fori_loop(1, nf, greet_feat, 0)

    for read in reads[:4]:
        read.wait()
    pay[my_feat, my_row, 0:quarter, :] = pred_ref[...]
    pay[my_feat, my_row, quarter : 2 * quarter, :] = (tie_ref[...] * 2 + event_ref[...]).astype(jnp.float32)
    share = node_ref[pl.ds(my_feat * quarter, quarter), :]
    pay[my_feat, my_row, 2 * quarter : 3 * quarter, :] = share.astype(jnp.float32)
    pl.semaphore_wait(barrier, nr + nf - 2)

    def row_copy(step):
        other = partner(my_row, step, nr)
        mine = pay.at[my_feat, my_row]
        return pltpu.make_async_remote_copy(
            src_ref=mine, dst_ref=mine, send_sem=row_send_sem, recv_sem=row_sem,
            device_id=(other, my_feat), device_id_type=MESH,
        )

    def feat_copy(step):
        other = (my_feat + step) % nf
        return pltpu.make_async_remote_copy(
            src_ref=pay.at[my_feat], dst_ref=pay.at[my_feat],
            send_sem=feat_send_sem, recv_sem=feat_sem,
            device_id=(my_row, other), device_id_type=MESH,
        )

    def bin_copy(step):
        other = partner(my_row, step, nr)
        return pltpu.make_async_remote_copy(
            src_ref=bin_send.at[other], dst_ref=bin_recv.at[my_row],
            send_sem=bin_send_sem.at[step], recv_sem=bin_sem.at[step],
            device_id=(other, my_feat), device_id_type=MESH,
        )

    def gain_copy(step, half):
        other = partner(my_row, step, nr)
        return pltpu.make_async_remote_copy(
            src_ref=gain_send.at[half, other], dst_ref=gain_recv.at[half, my_row],
            send_sem=gain_send_sem.at[half, step], recv_sem=gain_sem.at[half, step],
            device_id=(other, my_feat), device_id_type=MESH,
        )

    def send_row(step, carry):
        row_copy(nr - step).start()
        return carry

    lax.fori_loop(1, nr, send_row, 0)

    reads[4].wait()

    def pack(block, carry):
        lanes = pl.ds(pl.multiple_of(block * LANES, LANES), LANES)
        for target in range(nr):
            part = bin_ref[target * own : (target + 1) * own, lanes].astype(jnp.float32)
            if own < tile:
                part = jnp.concatenate([part, jnp.zeros((tile - own, LANES), jnp.float32)], axis=0)
            bin_send[target, block] = part.astype(jnp.bfloat16)
        return carry

    lax.fori_loop(0, blocks, pack, 0)

    def send_bins(place, carry):
        bin_copy(step_of(place, nr)).start()
        return carry

    lax.fori_loop(1, nr, send_bins, 0)

    bin_recv[my_row] = bin_send[my_row]
    acc[...] = jnp.zeros_like(acc)

    row_bytes = pay.at[0, pl.ds(0, nr - 1)]
    feat_bytes = pay.at[pl.ds(0, nf - 1)]
    pltpu.make_async_copy(row_bytes, row_bytes, row_sem).wait()

    def send_feat(step, carry):
        feat_copy(step).start()
        return carry

    lax.fori_loop(1, nf, send_feat, 0)
    pltpu.make_async_copy(feat_bytes, feat_bytes, feat_sem).wait()

    def spread(row, carry):
        for feat in range(nf):
            rows = pl.ds((row * nf + feat) * quarter, quarter)
            score[rows, :] = pay[feat, row, 0:quarter, :]
            code[rows, :] = pay[feat, row, quarter : 2 * quarter, :].astype(jnp.int32)
            levelled[rows, :] = pay[feat, row, 2 * quarter : 3 * quarter, :]
        return carry

    lax.fori_loop(0, nr, spread, 0)
    gradient, hessian = cox(score[...], code[...])
    grads[...] = gradient
    hesss[...] = hessian
    mine = pl.ds(me * quarter, quarter)
    grad_ref[...] = grads[mine, :]
    hess_ref[...] = hesss[mine, :]

    levels = lax.broadcasted_iota(jnp.int32, (NODES, LANES), 0).astype(jnp.float32)
    low_levels = [
        (lax.broadcasted_iota(jnp.int32, (16, LANES), 0) + 16 * part).astype(jnp.float32).astype(jnp.bfloat16)
        for part in range(LOW // 16)
    ]
    one = jnp.ones((16, LANES), jnp.bfloat16)
    zero = jnp.zeros((16, LANES), jnp.bfloat16)
    halves = gain_send.shape[0]
    some = own // halves
    width = NODES * some
    short = slice_bins // halves

    def prepare(place, carry):
        step = step_of(place, nr)
        source = partner(my_row, step, nr)

        @pl.when(place > 0)
        def _():
            bin_copy(step).wait_recv()

        for inner in range(blocks):
            block = source * blocks + inner
            row = pl.ds(block, 1)
            is_node = jnp.broadcast_to(levelled[row, :], (NODES, LANES)) == levels
            weight = jnp.concatenate(
                [
                    jnp.where(is_node, jnp.broadcast_to(grads[row, :], (NODES, LANES)), 0.0),
                    jnp.where(is_node, jnp.broadcast_to(hesss[row, :], (NODES, LANES)), 0.0),
                ],
                axis=0,
            )
            weights[block] = weight.astype(jnp.bfloat16)
            bins = bin_recv[source, inner].astype(jnp.float32)
            high = jnp.floor(bins * (1.0 / LOW))
            highs[block] = high
            lows[block] = bins - high * LOW
        count_source(source, 0)
        return carry

    def count_source(source, half):
        def one_chunk(chunk, carry):
            here = [source * blocks + chunk * BLOCKS + inner for inner in range(BLOCKS)]
            weight = [weights[block] for block in here]

            def row_of(ref, block, feature):
                row = ref[block, feature : feature + 1, :]
                return jnp.broadcast_to(row, (16, LANES)).astype(jnp.bfloat16)

            for group in range(half * some // GROUP, (half + 1) * some // GROUP):
                left, right = [], []
                for inner in range(GROUP):
                    feature = group * GROUP + inner
                    high = [row_of(highs, block, feature) for block in here]
                    low = [row_of(lows, block, feature) for block in here]
                    for level in range(HIGH - 1):
                        left.append(
                            jnp.concatenate(
                                [jnp.where(h <= level, w, zero) for h, w in zip(high, weight)], axis=1
                            )
                        )
                    left.append(jnp.concatenate(weight, axis=1))
                    for level in low_levels:
                        right.append(
                            jnp.concatenate([jnp.where(l <= level, one, zero) for l in low], axis=1)
                        )
                acc[group] += lax.dot_general(
                    jnp.concatenate(left, axis=0),
                    jnp.concatenate(right, axis=0),
                    (((1,), (1,)), ((), ())),
                    preferred_element_type=jnp.float32,
                )
            return carry

        lax.fori_loop(0, blocks // BLOCKS, one_chunk, 0)

    def count_again(half, source, carry):
        count_source(source, half)
        return carry

    def send_gain(half, step, carry):
        gain_copy(nr - step, half).start()
        return carry

    def take_gain(half, step, carry):
        gain_copy(step, half).wait_recv()
        return carry

    def split(half):
        for place in range(some):
            group, inner = divmod(half * some + place, GROUP)
            columns = slice(inner * LOW, (inner + 1) * LOW)
            lefts, before, running = [], [None, None], [None, None]
            for level in range(HIGH):
                for stat in range(2):
                    top = ((inner * HIGH + level) * 2 + stat) * NODES
                    part = acc[group, top : top + NODES, columns]
                    lefts.append(running[stat] + (part - before[stat]) if level else part)
                    before[stat] = part
                    running[stat] = jnp.broadcast_to(part[:, LOW - 1 :], (NODES, LOW))
            grad_all, hess_all = running
            base = grad_all * grad_all / (hess_all + 1.0)
            for level in range(HIGH):
                grad_left, hess_left = lefts[2 * level], lefts[2 * level + 1]
                rest = grad_all - grad_left
                gain = (
                    grad_left * grad_left / (hess_left + 1.0)
                    + rest * rest / (hess_all - hess_left + 1.0)
                    - base
                )
                turned[half, level, pl.ds(place, NODES, stride=some), 0:LOW] = gain
        for level in range(HIGH):
            flipped = jnp.transpose(turned[half, level])
            for part in range(LOW // slice_bins):
                top = part * slice_bins
                pieces = [flipped[top + sub * short : top + (sub + 1) * short, :width] for sub in range(halves)]
                whole = jnp.concatenate(pieces, axis=1) if halves > 1 else flipped[top : top + slice_bins]
                gain_send[half, level * (LOW // slice_bins) + part] = whole

    def place_gain(half):
        for source in range(nr):
            for sub in range(halves):
                for node in range(NODES):
                    lanes = sub * width + node * some
                    column = source * own + half * some
                    gain_ref[node, sub * short : (sub + 1) * short, column : column + some] = gain_recv[
                        half, source, :, lanes : lanes + some
                    ]

    for half in range(halves):
        if half:
            lax.fori_loop(0, nr, functools.partial(count_again, half), 0)
        else:
            lax.fori_loop(0, nr, prepare, 0)
        split(half)
        lax.fori_loop(1, nr, functools.partial(send_gain, half), 0)
        gain_recv[half, my_row] = gain_send[half, my_row]
    for half in range(halves):
        lax.fori_loop(1, nr, functools.partial(take_gain, half), 0)
        place_gain(half)

    def settle(step, carry):
        bin_copy(step).wait_send()
        for half in range(halves):
            gain_copy(step, half).wait_send()
        return carry

    lax.fori_loop(1, nr, settle, 0)
    pltpu.make_async_copy(row_bytes, row_bytes, row_send_sem).wait()
    pltpu.make_async_copy(feat_bytes, feat_bytes, feat_send_sem).wait()


def hand_on(*refs):
    count = len(refs) // 2
    copies = [
        pltpu.make_async_copy(refs[place], refs[count + place], refs[-1].at[place]) for place in range(count)
    ]
    for copy in copies:
        copy.start()
    for copy in copies:
        copy.wait()


def shards(nr, nf, predictor, events, tie_groups, node_ids, bin_index):
    length = predictor.shape[0]
    quarter = length // LANES
    rows = node_ids.shape[0]
    features = bin_index.shape[0]
    own = features // nr
    blocks = rows // LANES
    tile = -(-own // 16) * 16
    groups = -(-own // GROUP)
    all_rows = nr * blocks
    slice_bins = BINS // nr
    halves = 2 if own % (2 * GROUP) == 0 and NODES * own == LANES and slice_bins % 16 == 0 else 1
    vmem = pl.BlockSpec(memory_space=pltpu.VMEM)
    f32, bf16 = jnp.float32, jnp.bfloat16
    results = pl.pallas_call(
        functools.partial(kernel, nr, nf),
        out_shape=(
            jax.ShapeDtypeStruct((quarter, LANES), f32),
            jax.ShapeDtypeStruct((quarter, LANES), f32),
            jax.ShapeDtypeStruct((NODES, slice_bins, features), f32),
        ),
        in_specs=[pl.BlockSpec(memory_space=pltpu.HBM)] * 5,
        out_specs=(vmem,) * 3,
        scratch_shapes=[
            pltpu.VMEM((quarter, LANES), f32),
            pltpu.VMEM((quarter, LANES), jnp.int32),
            pltpu.VMEM((quarter, LANES), jnp.int32),
            pltpu.VMEM((blocks, LANES), jnp.int32),
            pltpu.VMEM((features, rows), jnp.int32),
            pltpu.VMEM((all_rows, tile, LANES), f32),
            pltpu.VMEM((all_rows, tile, LANES), f32),
            pltpu.VMEM((all_rows, CHANNELS, LANES), bf16),
            pltpu.VMEM((nf, nr, -(-3 * quarter // 8) * 8, LANES), f32),
            pltpu.VMEM((nr, blocks, tile, LANES), bf16),
            pltpu.VMEM((nr, blocks, tile, LANES), bf16),
            pltpu.VMEM((halves, nr, slice_bins // halves, LANES), f32),
            pltpu.VMEM((halves, nr, slice_bins // halves, LANES), f32),
            pltpu.VMEM((groups, GROUP * HIGH * CHANNELS, GROUP * LOW), f32),
            pltpu.VMEM((halves, HIGH, LANES, LANES), f32),
            pltpu.VMEM((all_rows, LANES), f32),
            pltpu.VMEM((all_rows, LANES), jnp.int32),
            pltpu.VMEM((all_rows, LANES), f32),
            pltpu.VMEM((all_rows, LANES), f32),
            pltpu.VMEM((all_rows, LANES), f32),
            pltpu.SemaphoreType.DMA((5,)),
            pltpu.SemaphoreType.DMA,
            pltpu.SemaphoreType.DMA,
            pltpu.SemaphoreType.DMA,
            pltpu.SemaphoreType.DMA,
            pltpu.SemaphoreType.DMA((nr,)),
            pltpu.SemaphoreType.DMA((nr,)),
            pltpu.SemaphoreType.DMA((halves, nr)),
            pltpu.SemaphoreType.DMA((halves, nr)),
        ],
        compiler_params=pltpu.CompilerParams(
            collective_id=0, has_side_effects=True, vmem_limit_bytes=63 * 1024 * 1024
        ),
    )(
        predictor.reshape(quarter, LANES),
        events.reshape(quarter, LANES),
        tie_groups.reshape(quarter, LANES),
        node_ids.reshape(blocks, LANES),
        bin_index,
    )
    hbm = pl.BlockSpec(memory_space=pltpu.HBM)
    gradient, hessian, gain = pl.pallas_call(
        hand_on,
        out_shape=tuple(jax.ShapeDtypeStruct(a.shape, a.dtype) for a in results),
        in_specs=[hbm] * 3,
        out_specs=(hbm,) * 3,
        scratch_shapes=[pltpu.SemaphoreType.DMA((3,))],
        compiler_params=pltpu.CompilerParams(vmem_limit_bytes=63 * 1024 * 1024),
    )(*results)
    return gradient.reshape(length), hessian.reshape(length), gain.transpose(0, 2, 1)


def solution(mesh):
    return jax.shard_map(
        functools.partial(shards, mesh.shape["row"], mesh.shape["feat"]),
        mesh=mesh,
        in_specs=(
            P(("row", "feat")),
            P(("row", "feat")),
            P(("row", "feat")),
            P("row"),
            P("feat", "row"),
        ),
        out_specs=(P(("row", "feat")), P(("row", "feat")), P(None, "feat", "row")),
        check_vma=False,
    )
```

```python
import functools

import jax
import jax.numpy as jnp
from jax import lax
from jax.experimental import pallas as pl
from jax.experimental.pallas import tpu as pltpu
from jax.sharding import PartitionSpec as P

BINS = 256
NODES = 8
LANES = 128
HIGH = 4
LOW = BINS // HIGH
CHANNELS = 2 * NODES
GROUP = 2
BLOCKS = 8
MESH = pl.DeviceIdType.MESH
EXACT = lax.Precision.HIGHEST


def partner(me, step, count):
    other = me
    bit = 1
    while bit < count:
        other = other + ((step // bit) % 2) * bit * (1 - 2 * ((me // bit) % 2))
        bit *= 2
    return other


def step_of(place, count):
    half = count // 2
    odd = place % 2
    last = place // (count - 1)
    later = (place + count - 1) // count
    by_turns = odd * ((place + 1) // 2) + (1 - odd) * later * (half + place // 2 - 1)
    return (1 - last) * by_turns + last * (count - 1)


def triangle(rows, columns, keep):
    a = lax.broadcasted_iota(jnp.int32, (rows, columns), 0)
    b = lax.broadcasted_iota(jnp.int32, (rows, columns), 1)
    return keep(a, b).astype(jnp.float32)


def exact_dot(a, b):
    return jnp.dot(a, b, precision=EXACT, preferred_element_type=jnp.float32)


def fill(value, known, step):
    for distance in (1, 2, 4):
        shift = distance if step > 0 else LANES - distance
        value = jnp.where(known > 0, value, pltpu.roll(value, shift, 1))
        known = jnp.maximum(known, pltpu.roll(known, shift, 1))
    return value


def cox(score, code):
    rows = score.shape[0]
    hazard_exp = jnp.exp(score)
    tie = code // 2
    failed = (code - 2 * tie).astype(jnp.float32)
    lane = lax.broadcasted_iota(jnp.int32, (rows, LANES), 1)
    begins = ((lane % 8 == 0) | (tie != pltpu.roll(tie, 1, 1))).astype(jnp.float32)
    finish = pltpu.roll(begins, LANES - 1, 1)
    lane_suffix = exact_dot(hazard_exp, triangle(LANES, LANES, lambda a, b: a >= b))
    whole = jnp.broadcast_to(lane_suffix[:, :1], (rows, LANES))
    suffix = lane_suffix + exact_dot(triangle(rows, rows, lambda a, b: b > a), whole)
    risk_sum = fill(suffix, begins, 1)
    weight_one = failed / risk_sum
    weight_two = failed / (risk_sum * risk_sum)
    upper = triangle(LANES, LANES, lambda a, b: a <= b)
    earlier = triangle(rows, rows, lambda a, b: b < a)

    def running(weight):
        within = exact_dot(weight, upper)
        whole = jnp.broadcast_to(within[:, LANES - 1 :], (rows, LANES))
        return fill(within + exact_dot(earlier, whole), finish, -1)

    hazard_one = running(weight_one)
    hazard_two = running(weight_two)
    gradient = hazard_exp * hazard_one - failed
    hessian = hazard_exp * hazard_one - hazard_exp * hazard_exp * hazard_two
    return gradient, hessian


def kernel(
    nr, nf, pred_hbm, event_hbm, tie_hbm, node_hbm, bin_hbm, grad_ref, hess_ref, gain_ref,
    pred_ref, event_ref, tie_ref, node_ref, bin_ref, highs, lows, weights,
    pay, bin_send, bin_recv, gain_send, gain_recv, acc, turned, score, code, grads, hesss,
    levelled, in_sem, row_send_sem, row_sem, feat_send_sem, feat_sem, bin_send_sem, bin_sem, gain_send_sem, gain_sem,
):
    my_row = lax.axis_index("row")
    my_feat = lax.axis_index("feat")
    me = my_row * nf + my_feat
    quarter = pred_ref.shape[0]
    blocks = bin_ref.shape[1] // LANES
    own = bin_ref.shape[0] // nr
    tile = bin_send.shape[2]
    slice_bins = BINS // nr

    reads = [
        pltpu.make_async_copy(source, target, in_sem.at[place])
        for place, (source, target) in enumerate(
            [(pred_hbm, pred_ref), (event_hbm, event_ref), (tie_hbm, tie_ref), (node_hbm, node_ref), (bin_hbm, bin_ref)]
        )
    ]
    for read in reads:
        read.start()
    barrier = pltpu.get_barrier_semaphore()

    def greet_row(step, carry):
        other = (my_row + step) % nr
        pl.semaphore_signal(barrier, inc=1, device_id=(other, my_feat), device_id_type=MESH)
        return carry

    def greet_feat(step, carry):
        other = (my_feat + step) % nf
        pl.semaphore_signal(barrier, inc=1, device_id=(my_row, other), device_id_type=MESH)
        return carry

    lax.fori_loop(1, nr, greet_row, 0)
    lax.fori_loop(1, nf, greet_feat, 0)

    for read in reads[:4]:
        read.wait()
    pay[my_feat, my_row, 0:quarter, :] = pred_ref[...]
    pay[my_feat, my_row, quarter : 2 * quarter, :] = (tie_ref[...] * 2 + event_ref[...]).astype(jnp.float32)
    share = node_ref[pl.ds(my_feat * quarter, quarter), :]
    pay[my_feat, my_row, 2 * quarter : 3 * quarter, :] = share.astype(jnp.float32)
    pl.semaphore_wait(barrier, nr + nf - 2)

    def row_copy(step):
        other = partner(my_row, step, nr)
        mine = pay.at[my_feat, my_row]
        return pltpu.make_async_remote_copy(
            src_ref=mine, dst_ref=mine, send_sem=row_send_sem, recv_sem=row_sem,
            device_id=(other, my_feat), device_id_type=MESH,
        )

    def feat_copy(step):
        other = (my_feat + step) % nf
        return pltpu.make_async_remote_copy(
            src_ref=pay.at[my_feat], dst_ref=pay.at[my_feat],
            send_sem=feat_send_sem, recv_sem=feat_sem,
            device_id=(my_row, other), device_id_type=MESH,
        )

    def bin_copy(step):
        other = partner(my_row, step, nr)
        return pltpu.make_async_remote_copy(
            src_ref=bin_send.at[other], dst_ref=bin_recv.at[my_row],
            send_sem=bin_send_sem.at[step], recv_sem=bin_sem.at[step],
            device_id=(other, my_feat), device_id_type=MESH,
        )

    def gain_copy(step, half):
        other = partner(my_row, step, nr)
        return pltpu.make_async_remote_copy(
            src_ref=gain_send.at[half, other], dst_ref=gain_recv.at[half, my_row],
            send_sem=gain_send_sem.at[half, step], recv_sem=gain_sem.at[half, step],
            device_id=(other, my_feat), device_id_type=MESH,
        )

    def send_row(step, carry):
        row_copy(nr - step).start()
        return carry

    lax.fori_loop(1, nr, send_row, 0)

    reads[4].wait()

    def pack(block, carry):
        lanes = pl.ds(pl.multiple_of(block * LANES, LANES), LANES)
        for target in range(nr):
            part = bin_ref[target * own : (target + 1) * own, lanes].astype(jnp.float32)
            if own < tile:
                part = jnp.concatenate([part, jnp.zeros((tile - own, LANES), jnp.float32)], axis=0)
            bin_send[target, block] = part.astype(jnp.bfloat16)
        return carry

    lax.fori_loop(0, blocks, pack, 0)

    bin_recv[my_row] = bin_send[my_row]
    acc[...] = jnp.zeros_like(acc)

    row_bytes = pay.at[0, pl.ds(0, nr - 1)]
    feat_bytes = pay.at[pl.ds(0, nf - 1)]
    pltpu.make_async_copy(row_bytes, row_bytes, row_sem).wait()

    def send_feat(step, carry):
        feat_copy(step).start()
        return carry

    lax.fori_loop(1, nf, send_feat, 0)

    def send_bins(place, carry):
        bin_copy(step_of(place, nr)).start()
        return carry

    lax.fori_loop(1, nr, send_bins, 0)
    pltpu.make_async_copy(feat_bytes, feat_bytes, feat_sem).wait()

    def spread(row, carry):
        for feat in range(nf):
            rows = pl.ds((row * nf + feat) * quarter, quarter)
            score[rows, :] = pay[feat, row, 0:quarter, :]
            code[rows, :] = pay[feat, row, quarter : 2 * quarter, :].astype(jnp.int32)
            levelled[rows, :] = pay[feat, row, 2 * quarter : 3 * quarter, :]
        return carry

    lax.fori_loop(0, nr, spread, 0)
    gradient, hessian = cox(score[...], code[...])
    grads[...] = gradient
    hesss[...] = hessian
    mine = pl.ds(me * quarter, quarter)
    grad_ref[...] = grads[mine, :]
    hess_ref[...] = hesss[mine, :]

    levels = lax.broadcasted_iota(jnp.int32, (NODES, LANES), 0).astype(jnp.float32)
    low_levels = [
        (lax.broadcasted_iota(jnp.int32, (16, LANES), 0) + 16 * part).astype(jnp.float32).astype(jnp.bfloat16)
        for part in range(LOW // 16)
    ]
    one = jnp.ones((16, LANES), jnp.bfloat16)
    zero = jnp.zeros((16, LANES), jnp.bfloat16)
    halves = gain_send.shape[0]
    some = own // halves
    width = NODES * some
    short = slice_bins // halves

    def prepare(place, carry):
        step = step_of(place, nr)
        source = partner(my_row, step, nr)

        @pl.when(place > 0)
        def _():
            bin_copy(step).wait_recv()

        for inner in range(blocks):
            block = source * blocks + inner
            row = pl.ds(block, 1)
            is_node = jnp.broadcast_to(levelled[row, :], (NODES, LANES)) == levels
            weight = jnp.concatenate(
                [
                    jnp.where(is_node, jnp.broadcast_to(grads[row, :], (NODES, LANES)), 0.0),
                    jnp.where(is_node, jnp.broadcast_to(hesss[row, :], (NODES, LANES)), 0.0),
                ],
                axis=0,
            )
            weights[block] = weight.astype(jnp.bfloat16)
            bins = bin_recv[source, inner].astype(jnp.float32)
            high = jnp.floor(bins * (1.0 / LOW))
            highs[block] = high
            lows[block] = bins - high * LOW
        count_source(source, 0)
        return carry

    def count_source(source, half):
        def one_chunk(chunk, carry):
            here = [source * blocks + chunk * BLOCKS + inner for inner in range(BLOCKS)]
            weight = [weights[block] for block in here]

            def row_of(ref, block, feature):
                row = ref[block, feature : feature + 1, :]
                return jnp.broadcast_to(row, (16, LANES)).astype(jnp.bfloat16)

            for group in range(half * some // GROUP, (half + 1) * some // GROUP):
                left, right = [], []
                for inner in range(GROUP):
                    feature = group * GROUP + inner
                    high = [row_of(highs, block, feature) for block in here]
                    low = [row_of(lows, block, feature) for block in here]
                    for level in range(HIGH - 1):
                        left.append(
                            jnp.concatenate(
                                [jnp.where(h <= level, w, zero) for h, w in zip(high, weight)], axis=1
                            )
                        )
                    left.append(jnp.concatenate(weight, axis=1))
                    for level in low_levels:
                        right.append(
                            jnp.concatenate([jnp.where(l <= level, one, zero) for l in low], axis=1)
                        )
                acc[group] += lax.dot_general(
                    jnp.concatenate(left, axis=0),
                    jnp.concatenate(right, axis=0),
                    (((1,), (1,)), ((), ())),
                    preferred_element_type=jnp.float32,
                )
            return carry

        lax.fori_loop(0, blocks // BLOCKS, one_chunk, 0)

    def count_again(half, source, carry):
        count_source(source, half)
        return carry

    def send_gain(half, step, carry):
        gain_copy(nr - step, half).start()
        return carry

    def take_gain(half, step, carry):
        gain_copy(step, half).wait_recv()
        return carry

    def split(half):
        for place in range(some):
            group, inner = divmod(half * some + place, GROUP)
            columns = slice(inner * LOW, (inner + 1) * LOW)
            lefts, before, running = [], [None, None], [None, None]
            for level in range(HIGH):
                for stat in range(2):
                    top = ((inner * HIGH + level) * 2 + stat) * NODES
                    part = acc[group, top : top + NODES, columns]
                    lefts.append(running[stat] + (part - before[stat]) if level else part)
                    before[stat] = part
                    running[stat] = jnp.broadcast_to(part[:, LOW - 1 :], (NODES, LOW))
            grad_all, hess_all = running
            base = grad_all * grad_all / (hess_all + 1.0)
            for level in range(HIGH):
                grad_left, hess_left = lefts[2 * level], lefts[2 * level + 1]
                rest = grad_all - grad_left
                gain = (
                    grad_left * grad_left / (hess_left + 1.0)
                    + rest * rest / (hess_all - hess_left + 1.0)
                    - base
                )
                turned[half, level, pl.ds(place, NODES, stride=some), 0:LOW] = gain
        for level in range(HIGH):
            flipped = jnp.transpose(turned[half, level])
            for part in range(LOW // slice_bins):
                top = part * slice_bins
                pieces = [flipped[top + sub * short : top + (sub + 1) * short, :width] for sub in range(halves)]
                whole = jnp.concatenate(pieces, axis=1) if halves > 1 else flipped[top : top + slice_bins]
                gain_send[half, level * (LOW // slice_bins) + part] = whole

    def place_gain(half):
        for source in range(nr):
            for sub in range(halves):
                for node in range(NODES):
                    lanes = sub * width + node * some
                    column = source * own + half * some
                    gain_ref[node, sub * short : (sub + 1) * short, column : column + some] = gain_recv[
                        half, source, :, lanes : lanes + some
                    ]

    for half in range(halves):
        if half:
            lax.fori_loop(0, nr, functools.partial(count_again, half), 0)
        else:
            lax.fori_loop(0, nr, prepare, 0)
        split(half)
        lax.fori_loop(1, nr, functools.partial(send_gain, half), 0)
        gain_recv[half, my_row] = gain_send[half, my_row]
    for half in range(halves):
        lax.fori_loop(1, nr, functools.partial(take_gain, half), 0)
        place_gain(half)

    def settle(step, carry):
        bin_copy(step).wait_send()
        for half in range(halves):
            gain_copy(step, half).wait_send()
        return carry

    lax.fori_loop(1, nr, settle, 0)
    pltpu.make_async_copy(row_bytes, row_bytes, row_send_sem).wait()
    pltpu.make_async_copy(feat_bytes, feat_bytes, feat_send_sem).wait()


def hand_on(*refs):
    count = len(refs) // 3
    sems = refs[-1]
    reads, writes = [], []
    for place in range(count):
        source, target, held = refs[place], refs[count + place], refs[2 * count + place]
        reads.append(pltpu.make_async_copy(source, held, sems.at[0, place]))
        writes.append(pltpu.make_async_copy(held, target, sems.at[1, place]))
    for read in reads:
        read.start()
    for read, write in zip(reads, writes):
        read.wait()
        write.start()
    for write in writes:
        write.wait()


def shards(nr, nf, predictor, events, tie_groups, node_ids, bin_index):
    length = predictor.shape[0]
    quarter = length // LANES
    rows = node_ids.shape[0]
    features = bin_index.shape[0]
    own = features // nr
    blocks = rows // LANES
    tile = -(-own // 16) * 16
    groups = -(-own // GROUP)
    all_rows = nr * blocks
    slice_bins = BINS // nr
    halves = 1
    vmem = pl.BlockSpec(memory_space=pltpu.VMEM)
    f32, bf16 = jnp.float32, jnp.bfloat16
    results = pl.pallas_call(
        functools.partial(kernel, nr, nf),
        out_shape=(
            jax.ShapeDtypeStruct((quarter, LANES), f32),
            jax.ShapeDtypeStruct((quarter, LANES), f32),
            jax.ShapeDtypeStruct((NODES, slice_bins, features), f32),
        ),
        in_specs=[pl.BlockSpec(memory_space=pltpu.HBM)] * 5,
        out_specs=(vmem,) * 3,
        scratch_shapes=[
            pltpu.VMEM((quarter, LANES), f32),
            pltpu.VMEM((quarter, LANES), jnp.int32),
            pltpu.VMEM((quarter, LANES), jnp.int32),
            pltpu.VMEM((blocks, LANES), jnp.int32),
            pltpu.VMEM((features, rows), jnp.int32),
            pltpu.VMEM((all_rows, tile, LANES), f32),
            pltpu.VMEM((all_rows, tile, LANES), f32),
            pltpu.VMEM((all_rows, CHANNELS, LANES), bf16),
            pltpu.VMEM((nf, nr, -(-3 * quarter // 8) * 8, LANES), f32),
            pltpu.VMEM((nr, blocks, tile, LANES), bf16),
            pltpu.VMEM((nr, blocks, tile, LANES), bf16),
            pltpu.VMEM((halves, nr, slice_bins // halves, LANES), f32),
            pltpu.VMEM((halves, nr, slice_bins // halves, LANES), f32),
            pltpu.VMEM((groups, GROUP * HIGH * CHANNELS, GROUP * LOW), f32),
            pltpu.VMEM((halves, HIGH, LANES, LANES), f32),
            pltpu.VMEM((all_rows, LANES), f32),
            pltpu.VMEM((all_rows, LANES), jnp.int32),
            pltpu.VMEM((all_rows, LANES), f32),
            pltpu.VMEM((all_rows, LANES), f32),
            pltpu.VMEM((all_rows, LANES), f32),
            pltpu.SemaphoreType.DMA((5,)),
            pltpu.SemaphoreType.DMA,
            pltpu.SemaphoreType.DMA,
            pltpu.SemaphoreType.DMA,
            pltpu.SemaphoreType.DMA,
            pltpu.SemaphoreType.DMA((nr,)),
            pltpu.SemaphoreType.DMA((nr,)),
            pltpu.SemaphoreType.DMA((halves, nr)),
            pltpu.SemaphoreType.DMA((halves, nr)),
        ],
        compiler_params=pltpu.CompilerParams(
            collective_id=0, has_side_effects=True, vmem_limit_bytes=63 * 1024 * 1024
        ),
    )(
        predictor.reshape(quarter, LANES),
        events.reshape(quarter, LANES),
        tie_groups.reshape(quarter, LANES),
        node_ids.reshape(blocks, LANES),
        bin_index,
    )
    hbm = pl.BlockSpec(memory_space=pltpu.HBM)
    gradient, hessian, gain = pl.pallas_call(
        hand_on,
        out_shape=tuple(jax.ShapeDtypeStruct(a.shape, a.dtype) for a in results),
        in_specs=[hbm] * 3,
        out_specs=(hbm,) * 3,
        scratch_shapes=[pltpu.VMEM(a.shape, a.dtype) for a in results] + [pltpu.SemaphoreType.DMA((2, 3))],
        compiler_params=pltpu.CompilerParams(vmem_limit_bytes=63 * 1024 * 1024),
    )(*results)
    return gradient.reshape(length), hessian.reshape(length), gain.transpose(0, 2, 1)


def solution(mesh):
    return jax.shard_map(
        functools.partial(shards, mesh.shape["row"], mesh.shape["feat"]),
        mesh=mesh,
        in_specs=(
            P(("row", "feat")),
            P(("row", "feat")),
            P(("row", "feat")),
            P("row"),
            P("feat", "row"),
        ),
        out_specs=(P(("row", "feat")), P(("row", "feat")), P(None, "feat", "row")),
        check_vma=False,
    )
```

```python
import functools

import jax
import jax.numpy as jnp
from jax import lax
from jax.experimental import pallas as pl
from jax.experimental.pallas import tpu as pltpu
from jax.sharding import PartitionSpec as P

BINS = 256
NODES = 8
LANES = 128
HIGH = 4
LOW = BINS // HIGH
CHANNELS = 2 * NODES
GROUP = 2
BLOCKS = 8
EARLY = 2
MESH = pl.DeviceIdType.MESH
EXACT = lax.Precision.HIGHEST


def partner(me, step, count):
    other = me
    bit = 1
    while bit < count:
        other = other + ((step // bit) % 2) * bit * (1 - 2 * ((me // bit) % 2))
        bit *= 2
    return other


def triangle(rows, columns, keep):
    a = lax.broadcasted_iota(jnp.int32, (rows, columns), 0)
    b = lax.broadcasted_iota(jnp.int32, (rows, columns), 1)
    return keep(a, b).astype(jnp.float32)


def exact_dot(a, b):
    return jnp.dot(a, b, precision=EXACT, preferred_element_type=jnp.float32)


def fill(value, known, step):
    for distance in (1, 2, 4):
        shift = distance if step > 0 else LANES - distance
        value = jnp.where(known > 0, value, pltpu.roll(value, shift, 1))
        known = jnp.maximum(known, pltpu.roll(known, shift, 1))
    return value


def cox(score, code):
    rows = score.shape[0]
    hazard_exp = jnp.exp(score)
    tie = code // 2
    failed = (code - 2 * tie).astype(jnp.float32)
    lane = lax.broadcasted_iota(jnp.int32, (rows, LANES), 1)
    begins = ((lane % 8 == 0) | (tie != pltpu.roll(tie, 1, 1))).astype(jnp.float32)
    finish = pltpu.roll(begins, LANES - 1, 1)
    lane_suffix = exact_dot(hazard_exp, triangle(LANES, LANES, lambda a, b: a >= b))
    whole = jnp.broadcast_to(lane_suffix[:, :1], (rows, LANES))
    suffix = lane_suffix + exact_dot(triangle(rows, rows, lambda a, b: b > a), whole)
    risk_sum = fill(suffix, begins, 1)
    weight_one = failed / risk_sum
    weight_two = failed / (risk_sum * risk_sum)
    upper = triangle(LANES, LANES, lambda a, b: a <= b)
    earlier = triangle(rows, rows, lambda a, b: b < a)

    def running(weight):
        within = exact_dot(weight, upper)
        whole = jnp.broadcast_to(within[:, LANES - 1 :], (rows, LANES))
        return fill(within + exact_dot(earlier, whole), finish, -1)

    hazard_one = running(weight_one)
    hazard_two = running(weight_two)
    gradient = hazard_exp * hazard_one - failed
    hessian = hazard_exp * hazard_one - hazard_exp * hazard_exp * hazard_two
    return gradient, hessian


def kernel(
    nr, nf, pred_hbm, event_hbm, tie_hbm, node_hbm, bin_hbm, grad_ref, hess_ref, gain_ref,
    pred_ref, event_ref, tie_ref, node_ref, bin_ref, highs, lows, weights,
    pay, bin_send, bin_recv, gain_send, gain_recv, acc, turned, score, code, grads, hesss,
    levelled, in_sem, row_send_sem, row_sem, feat_send_sem, feat_sem, bin_send_sem, bin_sem, gain_send_sem, gain_sem,
):
    my_row = lax.axis_index("row")
    my_feat = lax.axis_index("feat")
    me = my_row * nf + my_feat
    quarter = pred_ref.shape[0]
    blocks = bin_ref.shape[1] // LANES
    own = bin_ref.shape[0] // nr
    tile = bin_send.shape[2]
    slice_bins = BINS // nr

    reads = [
        pltpu.make_async_copy(source, target, in_sem.at[place])
        for place, (source, target) in enumerate(
            [(pred_hbm, pred_ref), (event_hbm, event_ref), (tie_hbm, tie_ref), (node_hbm, node_ref), (bin_hbm, bin_ref)]
        )
    ]
    for read in reads:
        read.start()
    barrier = pltpu.get_barrier_semaphore()

    def greet_row(step, carry):
        other = (my_row + step) % nr
        pl.semaphore_signal(barrier, inc=1, device_id=(other, my_feat), device_id_type=MESH)
        return carry

    def greet_feat(step, carry):
        other = (my_feat + step) % nf
        pl.semaphore_signal(barrier, inc=1, device_id=(my_row, other), device_id_type=MESH)
        return carry

    lax.fori_loop(1, nr, greet_row, 0)
    lax.fori_loop(1, nf, greet_feat, 0)

    for read in reads[:4]:
        read.wait()
    pay[my_feat, my_row, 0:quarter, :] = pred_ref[...]
    pay[my_feat, my_row, quarter : 2 * quarter, :] = (tie_ref[...] * 2 + event_ref[...]).astype(jnp.float32)
    share = node_ref[pl.ds(my_feat * quarter, quarter), :]
    pay[my_feat, my_row, 2 * quarter : 3 * quarter, :] = share.astype(jnp.float32)
    pl.semaphore_wait(barrier, nr + nf - 2)

    def row_copy(step):
        other = partner(my_row, step, nr)
        mine = pay.at[my_feat, my_row]
        return pltpu.make_async_remote_copy(
            src_ref=mine, dst_ref=mine, send_sem=row_send_sem, recv_sem=row_sem,
            device_id=(other, my_feat), device_id_type=MESH,
        )

    def feat_copy(step):
        other = (my_feat + step) % nf
        return pltpu.make_async_remote_copy(
            src_ref=pay.at[my_feat], dst_ref=pay.at[my_feat],
            send_sem=feat_send_sem, recv_sem=feat_sem,
            device_id=(my_row, other), device_id_type=MESH,
        )

    def bin_copy(step):
        other = partner(my_row, step, nr)
        return pltpu.make_async_remote_copy(
            src_ref=bin_send.at[other], dst_ref=bin_recv.at[my_row],
            send_sem=bin_send_sem.at[step], recv_sem=bin_sem.at[step],
            device_id=(other, my_feat), device_id_type=MESH,
        )

    def gain_copy(step, half):
        other = partner(my_row, step, nr)
        return pltpu.make_async_remote_copy(
            src_ref=gain_send.at[half, other], dst_ref=gain_recv.at[half, my_row],
            send_sem=gain_send_sem.at[half, step], recv_sem=gain_sem.at[half, step],
            device_id=(other, my_feat), device_id_type=MESH,
        )

    def send_row(step, carry):
        row_copy(nr - step).start()
        return carry

    lax.fori_loop(1, nr, send_row, 0)

    reads[4].wait()

    def pack(block, carry):
        lanes = pl.ds(pl.multiple_of(block * LANES, LANES), LANES)
        for target in range(nr):
            part = bin_ref[target * own : (target + 1) * own, lanes].astype(jnp.float32)
            if own < tile:
                part = jnp.concatenate([part, jnp.zeros((tile - own, LANES), jnp.float32)], axis=0)
            bin_send[target, block] = part.astype(jnp.bfloat16)
        return carry

    lax.fori_loop(0, blocks, pack, 0)

    early = min(EARLY, nr - 1)

    def send_bins(step, carry):
        bin_copy(step).start()
        return carry

    lax.fori_loop(1, early + 1, send_bins, 0)

    bin_recv[my_row] = bin_send[my_row]
    acc[...] = jnp.zeros_like(acc)

    row_bytes = pay.at[0, pl.ds(0, nr - 1)]
    feat_bytes = pay.at[pl.ds(0, nf - 1)]
    pltpu.make_async_copy(row_bytes, row_bytes, row_sem).wait()

    def send_feat(step, carry):
        feat_copy(step).start()
        return carry

    lax.fori_loop(1, nf, send_feat, 0)

    lax.fori_loop(early + 1, nr, send_bins, 0)
    pltpu.make_async_copy(feat_bytes, feat_bytes, feat_sem).wait()

    def spread(row, carry):
        for feat in range(nf):
            rows = pl.ds((row * nf + feat) * quarter, quarter)
            score[rows, :] = pay[feat, row, 0:quarter, :]
            code[rows, :] = pay[feat, row, quarter : 2 * quarter, :].astype(jnp.int32)
            levelled[rows, :] = pay[feat, row, 2 * quarter : 3 * quarter, :]
        return carry

    lax.fori_loop(0, nr, spread, 0)
    gradient, hessian = cox(score[...], code[...])
    grads[...] = gradient
    hesss[...] = hessian
    mine = pl.ds(me * quarter, quarter)
    grad_ref[...] = grads[mine, :]
    hess_ref[...] = hesss[mine, :]

    levels = lax.broadcasted_iota(jnp.int32, (NODES, LANES), 0).astype(jnp.float32)
    low_levels = [
        (lax.broadcasted_iota(jnp.int32, (16, LANES), 0) + 16 * part).astype(jnp.float32).astype(jnp.bfloat16)
        for part in range(LOW // 16)
    ]
    one = jnp.ones((16, LANES), jnp.bfloat16)
    zero = jnp.zeros((16, LANES), jnp.bfloat16)
    halves = gain_send.shape[0]
    some = own // halves
    width = NODES * some
    short = slice_bins // halves

    def prepare(step):
        source = partner(my_row, step, nr)

        @pl.when(step > 0)
        def _():
            bin_copy(step).wait_recv()

        for inner in range(blocks):
            block = source * blocks + inner
            row = pl.ds(block, 1)
            is_node = jnp.broadcast_to(levelled[row, :], (NODES, LANES)) == levels
            weight = jnp.concatenate(
                [
                    jnp.where(is_node, jnp.broadcast_to(grads[row, :], (NODES, LANES)), 0.0),
                    jnp.where(is_node, jnp.broadcast_to(hesss[row, :], (NODES, LANES)), 0.0),
                ],
                axis=0,
            )
            weights[block] = weight.astype(jnp.bfloat16)
            bins = bin_recv[source, inner].astype(jnp.float32)
            high = jnp.floor(bins * (1.0 / LOW))
            highs[block] = high
            lows[block] = bins - high * LOW
        return source

    def count_source(source, half):
        def one_chunk(chunk, carry):
            here = [source * blocks + chunk * BLOCKS + inner for inner in range(BLOCKS)]
            weight = [weights[block] for block in here]

            def row_of(ref, block, feature):
                row = ref[block, feature : feature + 1, :]
                return jnp.broadcast_to(row, (16, LANES)).astype(jnp.bfloat16)

            for group in range(half * some // GROUP, (half + 1) * some // GROUP):
                left, right = [], []
                for inner in range(GROUP):
                    feature = group * GROUP + inner
                    high = [row_of(highs, block, feature) for block in here]
                    low = [row_of(lows, block, feature) for block in here]
                    for level in range(HIGH - 1):
                        left.append(
                            jnp.concatenate(
                                [jnp.where(h <= level, w, zero) for h, w in zip(high, weight)], axis=1
                            )
                        )
                    left.append(jnp.concatenate(weight, axis=1))
                    for level in low_levels:
                        right.append(
                            jnp.concatenate([jnp.where(l <= level, one, zero) for l in low], axis=1)
                        )
                acc[group] += lax.dot_general(
                    jnp.concatenate(left, axis=0),
                    jnp.concatenate(right, axis=0),
                    (((1,), (1,)), ((), ())),
                    preferred_element_type=jnp.float32,
                )
            return carry

        lax.fori_loop(0, blocks // BLOCKS, one_chunk, 0)

    def count_all(step, carry):
        source = prepare(step)
        for half in range(halves):
            count_source(source, half)
        return carry

    def send_gain(half, step, carry):
        gain_copy(nr - step, half).start()
        return carry

    def take_gain(half, step, carry):
        gain_copy(step, half).wait_recv()
        return carry

    def split(half):
        for place in range(some):
            group, inner = divmod(half * some + place, GROUP)
            columns = slice(inner * LOW, (inner + 1) * LOW)
            lefts, before, running = [], [None, None], [None, None]
            for level in range(HIGH):
                for stat in range(2):
                    top = ((inner * HIGH + level) * 2 + stat) * NODES
                    part = acc[group, top : top + NODES, columns]
                    lefts.append(running[stat] + (part - before[stat]) if level else part)
                    before[stat] = part
                    running[stat] = jnp.broadcast_to(part[:, LOW - 1 :], (NODES, LOW))
            grad_all, hess_all = running
            base = grad_all * grad_all / (hess_all + 1.0)
            for level in range(HIGH):
                grad_left, hess_left = lefts[2 * level], lefts[2 * level + 1]
                rest = grad_all - grad_left
                gain = (
                    grad_left * grad_left / (hess_left + 1.0)
                    + rest * rest / (hess_all - hess_left + 1.0)
                    - base
                )
                turned[half, level, pl.ds(place, NODES, stride=some), 0:LOW] = gain
        for level in range(HIGH):
            flipped = jnp.transpose(turned[half, level])
            for part in range(LOW // slice_bins):
                top = part * slice_bins
                pieces = [flipped[top + sub * short : top + (sub + 1) * short, :width] for sub in range(halves)]
                whole = jnp.concatenate(pieces, axis=1) if halves > 1 else flipped[top : top + slice_bins]
                gain_send[half, level * (LOW // slice_bins) + part] = whole

    def place_gain(half):
        for source in range(nr):
            for sub in range(halves):
                for node in range(NODES):
                    lanes = sub * width + node * some
                    column = source * own + half * some
                    gain_ref[node, sub * short : (sub + 1) * short, column : column + some] = gain_recv[
                        half, source, :, lanes : lanes + some
                    ]

    lax.fori_loop(0, nr - 1, count_all, 0)
    last = prepare(jnp.int32(nr - 1))
    for half in range(halves):
        count_source(last, half)
        split(half)
        lax.fori_loop(1, nr, functools.partial(send_gain, half), 0)
        gain_recv[half, my_row] = gain_send[half, my_row]
    for half in range(halves):
        lax.fori_loop(1, nr, functools.partial(take_gain, half), 0)
        place_gain(half)

    def settle(step, carry):
        bin_copy(step).wait_send()
        for half in range(halves):
            gain_copy(step, half).wait_send()
        return carry

    lax.fori_loop(1, nr, settle, 0)
    pltpu.make_async_copy(row_bytes, row_bytes, row_send_sem).wait()
    pltpu.make_async_copy(feat_bytes, feat_bytes, feat_send_sem).wait()


def hand_on(*refs):
    count = len(refs) // 3
    sems = refs[-1]
    reads, writes = [], []
    for place in range(count):
        source, target, held = refs[place], refs[count + place], refs[2 * count + place]
        reads.append(pltpu.make_async_copy(source, held, sems.at[0, place]))
        writes.append(pltpu.make_async_copy(held, target, sems.at[1, place]))
    for read in reads:
        read.start()
    for read, write in zip(reads, writes):
        read.wait()
        write.start()
    for write in writes:
        write.wait()


def shards(nr, nf, predictor, events, tie_groups, node_ids, bin_index):
    length = predictor.shape[0]
    quarter = length // LANES
    rows = node_ids.shape[0]
    features = bin_index.shape[0]
    own = features // nr
    blocks = rows // LANES
    tile = -(-own // 16) * 16
    groups = -(-own // GROUP)
    all_rows = nr * blocks
    slice_bins = BINS // nr
    halves = 2 if own % (2 * GROUP) == 0 and NODES * own == LANES and slice_bins % 16 == 0 else 1
    vmem = pl.BlockSpec(memory_space=pltpu.VMEM)
    f32, bf16 = jnp.float32, jnp.bfloat16
    results = pl.pallas_call(
        functools.partial(kernel, nr, nf),
        out_shape=(
            jax.ShapeDtypeStruct((quarter, LANES), f32),
            jax.ShapeDtypeStruct((quarter, LANES), f32),
            jax.ShapeDtypeStruct((NODES, slice_bins, features), f32),
        ),
        in_specs=[pl.BlockSpec(memory_space=pltpu.HBM)] * 5,
        out_specs=(vmem,) * 3,
        scratch_shapes=[
            pltpu.VMEM((quarter, LANES), f32),
            pltpu.VMEM((quarter, LANES), jnp.int32),
            pltpu.VMEM((quarter, LANES), jnp.int32),
            pltpu.VMEM((blocks, LANES), jnp.int32),
            pltpu.VMEM((features, rows), jnp.int32),
            pltpu.VMEM((all_rows, tile, LANES), f32),
            pltpu.VMEM((all_rows, tile, LANES), f32),
            pltpu.VMEM((all_rows, CHANNELS, LANES), bf16),
            pltpu.VMEM((nf, nr, -(-3 * quarter // 8) * 8, LANES), f32),
            pltpu.VMEM((nr, blocks, tile, LANES), bf16),
            pltpu.VMEM((nr, blocks, tile, LANES), bf16),
            pltpu.VMEM((halves, nr, slice_bins // halves, LANES), f32),
            pltpu.VMEM((halves, nr, slice_bins // halves, LANES), f32),
            pltpu.VMEM((groups, GROUP * HIGH * CHANNELS, GROUP * LOW), f32),
            pltpu.VMEM((halves, HIGH, LANES, LANES), f32),
            pltpu.VMEM((all_rows, LANES), f32),
            pltpu.VMEM((all_rows, LANES), jnp.int32),
            pltpu.VMEM((all_rows, LANES), f32),
            pltpu.VMEM((all_rows, LANES), f32),
            pltpu.VMEM((all_rows, LANES), f32),
            pltpu.SemaphoreType.DMA((5,)),
            pltpu.SemaphoreType.DMA,
            pltpu.SemaphoreType.DMA,
            pltpu.SemaphoreType.DMA,
            pltpu.SemaphoreType.DMA,
            pltpu.SemaphoreType.DMA((nr,)),
            pltpu.SemaphoreType.DMA((nr,)),
            pltpu.SemaphoreType.DMA((halves, nr)),
            pltpu.SemaphoreType.DMA((halves, nr)),
        ],
        compiler_params=pltpu.CompilerParams(
            collective_id=0, has_side_effects=True, vmem_limit_bytes=63 * 1024 * 1024
        ),
    )(
        predictor.reshape(quarter, LANES),
        events.reshape(quarter, LANES),
        tie_groups.reshape(quarter, LANES),
        node_ids.reshape(blocks, LANES),
        bin_index,
    )
    hbm = pl.BlockSpec(memory_space=pltpu.HBM)
    gradient, hessian, gain = pl.pallas_call(
        hand_on,
        out_shape=tuple(jax.ShapeDtypeStruct(a.shape, a.dtype) for a in results),
        in_specs=[hbm] * 3,
        out_specs=(hbm,) * 3,
        scratch_shapes=[pltpu.VMEM(a.shape, a.dtype) for a in results] + [pltpu.SemaphoreType.DMA((2, 3))],
        compiler_params=pltpu.CompilerParams(vmem_limit_bytes=63 * 1024 * 1024),
    )(*results)
    return gradient.reshape(length), hessian.reshape(length), gain.transpose(0, 2, 1)


def solution(mesh):
    return jax.shard_map(
        functools.partial(shards, mesh.shape["row"], mesh.shape["feat"]),
        mesh=mesh,
        in_specs=(
            P(("row", "feat")),
            P(("row", "feat")),
            P(("row", "feat")),
            P("row"),
            P("feat", "row"),
        ),
        out_specs=(P(("row", "feat")), P(("row", "feat")), P(None, "feat", "row")),
        check_vma=False,
    )
```

```python
import functools

import jax
import jax.numpy as jnp
from jax import lax
from jax.experimental import pallas as pl
from jax.experimental.pallas import tpu as pltpu
from jax.sharding import PartitionSpec as P

BINS = 256
NODES = 8
LANES = 128
HIGH = 4
LOW = BINS // HIGH
CHANNELS = 2 * NODES
GROUP = 2
BLOCKS = 8
MESH = pl.DeviceIdType.MESH


def partner(me, step, count):
    other = me
    bit = 1
    while bit < count:
        other = other + ((step // bit) % 2) * bit * (1 - 2 * ((me // bit) % 2))
        bit *= 2
    return other


def step_of(place, count):
    half = count // 2
    odd = place % 2
    last = place // (count - 1)
    later = (place + count - 1) // count
    by_turns = odd * ((place + 1) // 2) + (1 - odd) * later * (half + place // 2 - 1)
    return (1 - last) * by_turns + last * (count - 1)


def triangle(rows, columns, keep):
    a = lax.broadcasted_iota(jnp.int32, (rows, columns), 0)
    b = lax.broadcasted_iota(jnp.int32, (rows, columns), 1)
    return keep(a, b).astype(jnp.float32).astype(jnp.bfloat16)


def thirds(value):
    parts = []
    for _ in range(3):
        part = value.astype(jnp.bfloat16)
        parts.append(part)
        value = value - part.astype(jnp.float32)
    return parts


def sum_lanes(values, keep):
    rows = values[0].shape[0]
    stacked = jnp.concatenate([part for value in values for part in thirds(value)], axis=0)
    product = jnp.dot(stacked, triangle(LANES, LANES, keep), preferred_element_type=jnp.float32)
    pieces = [product[place * rows : (place + 1) * rows] for place in range(3 * len(values))]
    return [pieces[3 * k] + (pieces[3 * k + 1] + pieces[3 * k + 2]) for k in range(len(values))]


def sum_rows(values, keep):
    rows = values[0].shape[0]
    stacked = jnp.concatenate([part for value in values for part in thirds(value)], axis=1)
    product = jnp.dot(triangle(rows, rows, keep), stacked, preferred_element_type=jnp.float32)
    pieces = [product[:, place * LANES : (place + 1) * LANES] for place in range(3 * len(values))]
    return [pieces[3 * k] + (pieces[3 * k + 1] + pieces[3 * k + 2]) for k in range(len(values))]


def fill(value, known, step):
    for distance in (1, 2, 4):
        shift = distance if step > 0 else LANES - distance
        value = jnp.where(known > 0, value, pltpu.roll(value, shift, 1))
        known = jnp.maximum(known, pltpu.roll(known, shift, 1))
    return value


def cox(score, code):
    rows = score.shape[0]
    hazard_exp = jnp.exp(score)
    tie = code // 2
    failed = (code - 2 * tie).astype(jnp.float32)
    lane = lax.broadcasted_iota(jnp.int32, (rows, LANES), 1)
    begins = ((lane % 8 == 0) | (tie != pltpu.roll(tie, 1, 1))).astype(jnp.float32)
    finish = pltpu.roll(begins, LANES - 1, 1)
    (lane_suffix,) = sum_lanes([hazard_exp], lambda a, b: a >= b)
    (later,) = sum_rows([jnp.broadcast_to(lane_suffix[:, :1], (rows, LANES))], lambda a, b: b > a)
    suffix = lane_suffix + later
    risk_sum = fill(suffix, begins, 1)
    weight_one = failed / risk_sum
    weight_two = failed / (risk_sum * risk_sum)
    within = sum_lanes([weight_one, weight_two], lambda a, b: a <= b)
    wholes = [jnp.broadcast_to(w[:, LANES - 1 :], (rows, LANES)) for w in within]
    before = sum_rows(wholes, lambda a, b: b < a)
    hazard_one = fill(within[0] + before[0], finish, -1)
    hazard_two = fill(within[1] + before[1], finish, -1)
    gradient = hazard_exp * hazard_one - failed
    hessian = hazard_exp * hazard_one - hazard_exp * hazard_exp * hazard_two
    return gradient, hessian


def kernel(
    nr, nf, pred_hbm, event_hbm, tie_hbm, node_hbm, bin_hbm, grad_ref, hess_ref, gain_ref,
    pred_ref, event_ref, tie_ref, node_ref, bin_ref, highs, lows, weights,
    pay, bin_send, bin_recv, gain_send, gain_recv, acc, turned, score, code, grads, hesss,
    levelled, in_sem, row_send_sem, row_sem, feat_send_sem, feat_sem, bin_send_sem, bin_sem, gain_send_sem, gain_sem,
):
    my_row = lax.axis_index("row")
    my_feat = lax.axis_index("feat")
    me = my_row * nf + my_feat
    quarter = pred_ref.shape[0]
    blocks = bin_ref.shape[1] // LANES
    own = bin_ref.shape[0] // nr
    tile = bin_send.shape[2]
    slice_bins = BINS // nr

    reads = [
        pltpu.make_async_copy(source, target, in_sem.at[place])
        for place, (source, target) in enumerate(
            [(pred_hbm, pred_ref), (event_hbm, event_ref), (tie_hbm, tie_ref), (node_hbm, node_ref), (bin_hbm, bin_ref)]
        )
    ]
    for read in reads:
        read.start()
    barrier = pltpu.get_barrier_semaphore()

    def greet_row(step, carry):
        other = (my_row + step) % nr
        pl.semaphore_signal(barrier, inc=1, device_id=(other, my_feat), device_id_type=MESH)
        return carry

    def greet_feat(step, carry):
        other = (my_feat + step) % nf
        pl.semaphore_signal(barrier, inc=1, device_id=(my_row, other), device_id_type=MESH)
        return carry

    lax.fori_loop(1, nr, greet_row, 0)
    lax.fori_loop(1, nf, greet_feat, 0)

    for read in reads[:4]:
        read.wait()
    pay[my_feat, my_row, 0:quarter, :] = pred_ref[...]
    pay[my_feat, my_row, quarter : 2 * quarter, :] = (tie_ref[...] * 2 + event_ref[...]).astype(jnp.float32)
    share = node_ref[pl.ds(my_feat * quarter, quarter), :]
    pay[my_feat, my_row, 2 * quarter : 3 * quarter, :] = share.astype(jnp.float32)
    pl.semaphore_wait(barrier, nr + nf - 2)

    def row_copy(step):
        other = partner(my_row, step, nr)
        mine = pay.at[my_feat, my_row]
        return pltpu.make_async_remote_copy(
            src_ref=mine, dst_ref=mine, send_sem=row_send_sem, recv_sem=row_sem,
            device_id=(other, my_feat), device_id_type=MESH,
        )

    def feat_copy(step):
        other = (my_feat + step) % nf
        return pltpu.make_async_remote_copy(
            src_ref=pay.at[my_feat], dst_ref=pay.at[my_feat],
            send_sem=feat_send_sem, recv_sem=feat_sem,
            device_id=(my_row, other), device_id_type=MESH,
        )

    def bin_copy(step):
        other = partner(my_row, step, nr)
        return pltpu.make_async_remote_copy(
            src_ref=bin_send.at[other], dst_ref=bin_recv.at[my_row],
            send_sem=bin_send_sem.at[step], recv_sem=bin_sem.at[step],
            device_id=(other, my_feat), device_id_type=MESH,
        )

    def gain_copy(step, half):
        other = partner(my_row, step, nr)
        return pltpu.make_async_remote_copy(
            src_ref=gain_send.at[half, other], dst_ref=gain_recv.at[half, my_row],
            send_sem=gain_send_sem.at[half, step], recv_sem=gain_sem.at[half, step],
            device_id=(other, my_feat), device_id_type=MESH,
        )

    def send_row(step, carry):
        row_copy(nr - step).start()
        return carry

    lax.fori_loop(1, nr, send_row, 0)

    reads[4].wait()

    def pack(block, carry):
        lanes = pl.ds(pl.multiple_of(block * LANES, LANES), LANES)
        for target in range(nr):
            part = bin_ref[target * own : (target + 1) * own, lanes].astype(jnp.float32)
            if own < tile:
                part = jnp.concatenate([part, jnp.zeros((tile - own, LANES), jnp.float32)], axis=0)
            bin_send[target, block] = part.astype(jnp.bfloat16)
        return carry

    lax.fori_loop(0, blocks, pack, 0)

    bin_recv[my_row] = bin_send[my_row]
    acc[...] = jnp.zeros_like(acc)

    row_bytes = pay.at[0, pl.ds(0, nr - 1)]
    feat_bytes = pay.at[pl.ds(0, nf - 1)]
    pltpu.make_async_copy(row_bytes, row_bytes, row_sem).wait()

    def send_feat(step, carry):
        feat_copy(step).start()
        return carry

    lax.fori_loop(1, nf, send_feat, 0)

    def send_bins(place, carry):
        bin_copy(step_of(place, nr)).start()
        return carry

    lax.fori_loop(1, nr, send_bins, 0)
    pltpu.make_async_copy(feat_bytes, feat_bytes, feat_sem).wait()

    def spread(row, carry):
        for feat in range(nf):
            rows = pl.ds((row * nf + feat) * quarter, quarter)
            score[rows, :] = pay[feat, row, 0:quarter, :]
            code[rows, :] = pay[feat, row, quarter : 2 * quarter, :].astype(jnp.int32)
            levelled[rows, :] = pay[feat, row, 2 * quarter : 3 * quarter, :]
        return carry

    lax.fori_loop(0, nr, spread, 0)
    gradient, hessian = cox(score[...], code[...])
    grads[...] = gradient
    hesss[...] = hessian
    mine = pl.ds(me * quarter, quarter)
    grad_ref[...] = grads[mine, :]
    hess_ref[...] = hesss[mine, :]

    levels = lax.broadcasted_iota(jnp.int32, (NODES, LANES), 0).astype(jnp.float32)
    low_levels = [
        (lax.broadcasted_iota(jnp.int32, (16, LANES), 0) + 16 * part).astype(jnp.float32).astype(jnp.bfloat16)
        for part in range(LOW // 16)
    ]
    one = jnp.ones((16, LANES), jnp.bfloat16)
    zero = jnp.zeros((16, LANES), jnp.bfloat16)
    halves = gain_send.shape[0]
    some = own // halves
    width = NODES * some
    short = slice_bins // halves

    def prepare(place, carry):
        step = step_of(place, nr)
        source = partner(my_row, step, nr)

        @pl.when(place > 0)
        def _():
            bin_copy(step).wait_recv()

        for inner in range(blocks):
            block = source * blocks + inner
            row = pl.ds(block, 1)
            is_node = jnp.broadcast_to(levelled[row, :], (NODES, LANES)) == levels
            weight = jnp.concatenate(
                [
                    jnp.where(is_node, jnp.broadcast_to(grads[row, :], (NODES, LANES)), 0.0),
                    jnp.where(is_node, jnp.broadcast_to(hesss[row, :], (NODES, LANES)), 0.0),
                ],
                axis=0,
            )
            weights[block] = weight.astype(jnp.bfloat16)
            bins = bin_recv[source, inner].astype(jnp.float32)
            high = jnp.floor(bins * (1.0 / LOW))
            highs[block] = high
            lows[block] = bins - high * LOW
        count_source(source, 0)
        return carry

    def count_source(source, half):
        def one_chunk(chunk, carry):
            here = [source * blocks + chunk * BLOCKS + inner for inner in range(BLOCKS)]
            weight = [weights[block] for block in here]

            def row_of(ref, block, feature):
                row = ref[block, feature : feature + 1, :]
                return jnp.broadcast_to(row, (16, LANES)).astype(jnp.bfloat16)

            for group in range(half * some // GROUP, (half + 1) * some // GROUP):
                left, right = [], []
                for inner in range(GROUP):
                    feature = group * GROUP + inner
                    high = [row_of(highs, block, feature) for block in here]
                    low = [row_of(lows, block, feature) for block in here]
                    for level in range(HIGH - 1):
                        left.append(
                            jnp.concatenate(
                                [jnp.where(h <= level, w, zero) for h, w in zip(high, weight)], axis=1
                            )
                        )
                    left.append(jnp.concatenate(weight, axis=1))
                    for level in low_levels:
                        right.append(
                            jnp.concatenate([jnp.where(l <= level, one, zero) for l in low], axis=1)
                        )
                acc[group] += lax.dot_general(
                    jnp.concatenate(left, axis=0),
                    jnp.concatenate(right, axis=0),
                    (((1,), (1,)), ((), ())),
                    preferred_element_type=jnp.float32,
                )
            return carry

        lax.fori_loop(0, blocks // BLOCKS, one_chunk, 0)

    def count_again(half, source, carry):
        count_source(source, half)
        return carry

    def send_gain(half, step, carry):
        gain_copy(nr - step, half).start()
        return carry

    def take_gain(half, step, carry):
        gain_copy(step, half).wait_recv()
        return carry

    def split(half):
        for place in range(some):
            group, inner = divmod(half * some + place, GROUP)
            columns = slice(inner * LOW, (inner + 1) * LOW)
            lefts, before, running = [], [None, None], [None, None]
            for level in range(HIGH):
                for stat in range(2):
                    top = ((inner * HIGH + level) * 2 + stat) * NODES
                    part = acc[group, top : top + NODES, columns]
                    lefts.append(running[stat] + (part - before[stat]) if level else part)
                    before[stat] = part
                    running[stat] = jnp.broadcast_to(part[:, LOW - 1 :], (NODES, LOW))
            grad_all, hess_all = running
            base = grad_all * grad_all / (hess_all + 1.0)
            for level in range(HIGH):
                grad_left, hess_left = lefts[2 * level], lefts[2 * level + 1]
                rest = grad_all - grad_left
                gain = (
                    grad_left * grad_left / (hess_left + 1.0)
                    + rest * rest / (hess_all - hess_left + 1.0)
                    - base
                )
                turned[half, level, pl.ds(place, NODES, stride=some), 0:LOW] = gain
        for level in range(HIGH):
            flipped = jnp.transpose(turned[half, level])
            for part in range(LOW // slice_bins):
                top = part * slice_bins
                pieces = [flipped[top + sub * short : top + (sub + 1) * short, :width] for sub in range(halves)]
                whole = jnp.concatenate(pieces, axis=1) if halves > 1 else flipped[top : top + slice_bins]
                gain_send[half, level * (LOW // slice_bins) + part] = whole

    def place_gain(half):
        for source in range(nr):
            for sub in range(halves):
                for node in range(NODES):
                    lanes = sub * width + node * some
                    column = source * own + half * some
                    gain_ref[node, sub * short : (sub + 1) * short, column : column + some] = gain_recv[
                        half, source, :, lanes : lanes + some
                    ]

    for half in range(halves):
        if half:
            lax.fori_loop(0, nr, functools.partial(count_again, half), 0)
        else:
            lax.fori_loop(0, nr, prepare, 0)
        split(half)
        lax.fori_loop(1, nr, functools.partial(send_gain, half), 0)
        gain_recv[half, my_row] = gain_send[half, my_row]
    for half in range(halves):
        lax.fori_loop(1, nr, functools.partial(take_gain, half), 0)
        place_gain(half)

    def settle(step, carry):
        bin_copy(step).wait_send()
        for half in range(halves):
            gain_copy(step, half).wait_send()
        return carry

    lax.fori_loop(1, nr, settle, 0)
    pltpu.make_async_copy(row_bytes, row_bytes, row_send_sem).wait()
    pltpu.make_async_copy(feat_bytes, feat_bytes, feat_send_sem).wait()


def hand_on(*refs):
    count = len(refs) // 3
    sems = refs[-1]
    reads, writes = [], []
    for place in range(count):
        source, target, held = refs[place], refs[count + place], refs[2 * count + place]
        reads.append(pltpu.make_async_copy(source, held, sems.at[0, place]))
        writes.append(pltpu.make_async_copy(held, target, sems.at[1, place]))
    for read in reads:
        read.start()
    for read, write in zip(reads, writes):
        read.wait()
        write.start()
    for write in writes:
        write.wait()


def shards(nr, nf, predictor, events, tie_groups, node_ids, bin_index):
    length = predictor.shape[0]
    quarter = length // LANES
    rows = node_ids.shape[0]
    features = bin_index.shape[0]
    own = features // nr
    blocks = rows // LANES
    tile = -(-own // 16) * 16
    groups = -(-own // GROUP)
    all_rows = nr * blocks
    slice_bins = BINS // nr
    halves = 1
    vmem = pl.BlockSpec(memory_space=pltpu.VMEM)
    f32, bf16 = jnp.float32, jnp.bfloat16
    results = pl.pallas_call(
        functools.partial(kernel, nr, nf),
        out_shape=(
            jax.ShapeDtypeStruct((quarter, LANES), f32),
            jax.ShapeDtypeStruct((quarter, LANES), f32),
            jax.ShapeDtypeStruct((NODES, slice_bins, features), f32),
        ),
        in_specs=[pl.BlockSpec(memory_space=pltpu.HBM)] * 5,
        out_specs=(vmem,) * 3,
        scratch_shapes=[
            pltpu.VMEM((quarter, LANES), f32),
            pltpu.VMEM((quarter, LANES), jnp.int32),
            pltpu.VMEM((quarter, LANES), jnp.int32),
            pltpu.VMEM((blocks, LANES), jnp.int32),
            pltpu.VMEM((features, rows), jnp.int32),
            pltpu.VMEM((all_rows, tile, LANES), f32),
            pltpu.VMEM((all_rows, tile, LANES), f32),
            pltpu.VMEM((all_rows, CHANNELS, LANES), bf16),
            pltpu.VMEM((nf, nr, -(-3 * quarter // 8) * 8, LANES), f32),
            pltpu.VMEM((nr, blocks, tile, LANES), bf16),
            pltpu.VMEM((nr, blocks, tile, LANES), bf16),
            pltpu.VMEM((halves, nr, slice_bins // halves, LANES), f32),
            pltpu.VMEM((halves, nr, slice_bins // halves, LANES), f32),
            pltpu.VMEM((groups, GROUP * HIGH * CHANNELS, GROUP * LOW), f32),
            pltpu.VMEM((halves, HIGH, LANES, LANES), f32),
            pltpu.VMEM((all_rows, LANES), f32),
            pltpu.VMEM((all_rows, LANES), jnp.int32),
            pltpu.VMEM((all_rows, LANES), f32),
            pltpu.VMEM((all_rows, LANES), f32),
            pltpu.VMEM((all_rows, LANES), f32),
            pltpu.SemaphoreType.DMA((5,)),
            pltpu.SemaphoreType.DMA,
            pltpu.SemaphoreType.DMA,
            pltpu.SemaphoreType.DMA,
            pltpu.SemaphoreType.DMA,
            pltpu.SemaphoreType.DMA((nr,)),
            pltpu.SemaphoreType.DMA((nr,)),
            pltpu.SemaphoreType.DMA((halves, nr)),
            pltpu.SemaphoreType.DMA((halves, nr)),
        ],
        compiler_params=pltpu.CompilerParams(
            collective_id=0, has_side_effects=True, vmem_limit_bytes=63 * 1024 * 1024
        ),
    )(
        predictor.reshape(quarter, LANES),
        events.reshape(quarter, LANES),
        tie_groups.reshape(quarter, LANES),
        node_ids.reshape(blocks, LANES),
        bin_index,
    )
    hbm = pl.BlockSpec(memory_space=pltpu.HBM)
    gradient, hessian, gain = pl.pallas_call(
        hand_on,
        out_shape=tuple(jax.ShapeDtypeStruct(a.shape, a.dtype) for a in results),
        in_specs=[hbm] * 3,
        out_specs=(hbm,) * 3,
        scratch_shapes=[pltpu.VMEM(a.shape, a.dtype) for a in results] + [pltpu.SemaphoreType.DMA((2, 3))],
        compiler_params=pltpu.CompilerParams(vmem_limit_bytes=63 * 1024 * 1024),
    )(*results)
    return gradient.reshape(length), hessian.reshape(length), gain.transpose(0, 2, 1)


def solution(mesh):
    return jax.shard_map(
        functools.partial(shards, mesh.shape["row"], mesh.shape["feat"]),
        mesh=mesh,
        in_specs=(
            P(("row", "feat")),
            P(("row", "feat")),
            P(("row", "feat")),
            P("row"),
            P("feat", "row"),
        ),
        out_specs=(P(("row", "feat")), P(("row", "feat")), P(None, "feat", "row")),
        check_vma=False,
    )
```

```python
import functools

import jax
import jax.numpy as jnp
from jax import lax
from jax.experimental import pallas as pl
from jax.experimental.pallas import tpu as pltpu
from jax.sharding import PartitionSpec as P

BINS = 256
NODES = 8
LANES = 128
HIGH = 4
LOW = BINS // HIGH
CHANNELS = 2 * NODES
GROUP = 2
BLOCKS = 16
MESH = pl.DeviceIdType.MESH


def partner(me, step, count):
    other = me
    bit = 1
    while bit < count:
        other = other + ((step // bit) % 2) * bit * (1 - 2 * ((me // bit) % 2))
        bit *= 2
    return other


def step_of(place, count):
    half = count // 2
    odd = place % 2
    last = place // (count - 1)
    later = (place + count - 1) // count
    by_turns = odd * ((place + 1) // 2) + (1 - odd) * later * (half + place // 2 - 1)
    return (1 - last) * by_turns + last * (count - 1)


def triangle(rows, columns, keep):
    a = lax.broadcasted_iota(jnp.int32, (rows, columns), 0)
    b = lax.broadcasted_iota(jnp.int32, (rows, columns), 1)
    return keep(a, b).astype(jnp.float32).astype(jnp.bfloat16)


def thirds(value):
    parts = []
    for _ in range(3):
        part = value.astype(jnp.bfloat16)
        parts.append(part)
        value = value - part.astype(jnp.float32)
    return parts


def sum_lanes(values, keep):
    rows = values[0].shape[0]
    stacked = jnp.concatenate([part for value in values for part in thirds(value)], axis=0)
    product = jnp.dot(stacked, triangle(LANES, LANES, keep), preferred_element_type=jnp.float32)
    pieces = [product[place * rows : (place + 1) * rows] for place in range(3 * len(values))]
    return [pieces[3 * k] + (pieces[3 * k + 1] + pieces[3 * k + 2]) for k in range(len(values))]


def sum_rows(values, keep):
    rows = values[0].shape[0]
    stacked = jnp.concatenate([part for value in values for part in thirds(value)], axis=1)
    product = jnp.dot(triangle(rows, rows, keep), stacked, preferred_element_type=jnp.float32)
    pieces = [product[:, place * LANES : (place + 1) * LANES] for place in range(3 * len(values))]
    return [pieces[3 * k] + (pieces[3 * k + 1] + pieces[3 * k + 2]) for k in range(len(values))]


def fill(value, known, step):
    for distance in (1, 2, 4):
        shift = distance if step > 0 else LANES - distance
        value = jnp.where(known > 0, value, pltpu.roll(value, shift, 1))
        known = jnp.maximum(known, pltpu.roll(known, shift, 1))
    return value


def cox(score, code):
    rows = score.shape[0]
    hazard_exp = jnp.exp(score)
    tie = code // 2
    failed = (code - 2 * tie).astype(jnp.float32)
    lane = lax.broadcasted_iota(jnp.int32, (rows, LANES), 1)
    begins = ((lane % 8 == 0) | (tie != pltpu.roll(tie, 1, 1))).astype(jnp.float32)
    finish = pltpu.roll(begins, LANES - 1, 1)
    (lane_suffix,) = sum_lanes([hazard_exp], lambda a, b: a >= b)
    (later,) = sum_rows([jnp.broadcast_to(lane_suffix[:, :1], (rows, LANES))], lambda a, b: b > a)
    suffix = lane_suffix + later
    risk_sum = fill(suffix, begins, 1)
    weight_one = failed / risk_sum
    weight_two = failed / (risk_sum * risk_sum)
    within = sum_lanes([weight_one, weight_two], lambda a, b: a <= b)
    wholes = [jnp.broadcast_to(w[:, LANES - 1 :], (rows, LANES)) for w in within]
    before = sum_rows(wholes, lambda a, b: b < a)
    hazard_one = fill(within[0] + before[0], finish, -1)
    hazard_two = fill(within[1] + before[1], finish, -1)
    gradient = hazard_exp * hazard_one - failed
    hessian = hazard_exp * hazard_one - hazard_exp * hazard_exp * hazard_two
    return gradient, hessian


def kernel(
    nr, nf, pred_hbm, event_hbm, tie_hbm, node_hbm, bin_hbm, grad_ref, hess_ref, gain_ref,
    pred_ref, event_ref, tie_ref, node_ref, bin_ref, highs, lows, weights,
    pay, bin_send, bin_recv, gain_send, gain_recv, acc, turned, score, code, grads, hesss,
    levelled, in_sem, row_send_sem, row_sem, feat_send_sem, feat_sem, bin_send_sem, bin_sem, gain_send_sem, gain_sem,
):
    my_row = lax.axis_index("row")
    my_feat = lax.axis_index("feat")
    me = my_row * nf + my_feat
    quarter = pred_ref.shape[0]
    blocks = bin_ref.shape[1] // LANES
    own = bin_ref.shape[0] // nr
    tile = bin_send.shape[2]
    slice_bins = BINS // nr

    reads = [
        pltpu.make_async_copy(source, target, in_sem.at[place])
        for place, (source, target) in enumerate(
            [(pred_hbm, pred_ref), (event_hbm, event_ref), (tie_hbm, tie_ref), (node_hbm, node_ref), (bin_hbm, bin_ref)]
        )
    ]
    for read in reads:
        read.start()
    barrier = pltpu.get_barrier_semaphore()

    def greet_row(step, carry):
        other = (my_row + step) % nr
        pl.semaphore_signal(barrier, inc=1, device_id=(other, my_feat), device_id_type=MESH)
        return carry

    def greet_feat(step, carry):
        other = (my_feat + step) % nf
        pl.semaphore_signal(barrier, inc=1, device_id=(my_row, other), device_id_type=MESH)
        return carry

    lax.fori_loop(1, nr, greet_row, 0)
    lax.fori_loop(1, nf, greet_feat, 0)

    for read in reads[:4]:
        read.wait()
    pay[my_feat, my_row, 0:quarter, :] = pred_ref[...]
    pay[my_feat, my_row, quarter : 2 * quarter, :] = (tie_ref[...] * 2 + event_ref[...]).astype(jnp.float32)
    share = node_ref[pl.ds(my_feat * quarter, quarter), :]
    pay[my_feat, my_row, 2 * quarter : 3 * quarter, :] = share.astype(jnp.float32)
    pl.semaphore_wait(barrier, nr + nf - 2)

    def row_copy(step):
        other = partner(my_row, step, nr)
        mine = pay.at[my_feat, my_row]
        return pltpu.make_async_remote_copy(
            src_ref=mine, dst_ref=mine, send_sem=row_send_sem, recv_sem=row_sem,
            device_id=(other, my_feat), device_id_type=MESH,
        )

    def feat_copy(step):
        other = (my_feat + step) % nf
        return pltpu.make_async_remote_copy(
            src_ref=pay.at[my_feat], dst_ref=pay.at[my_feat],
            send_sem=feat_send_sem, recv_sem=feat_sem,
            device_id=(my_row, other), device_id_type=MESH,
        )

    def bin_copy(step):
        other = partner(my_row, step, nr)
        return pltpu.make_async_remote_copy(
            src_ref=bin_send.at[other], dst_ref=bin_recv.at[my_row],
            send_sem=bin_send_sem.at[step], recv_sem=bin_sem.at[step],
            device_id=(other, my_feat), device_id_type=MESH,
        )

    def gain_copy(step, half):
        other = partner(my_row, step, nr)
        return pltpu.make_async_remote_copy(
            src_ref=gain_send.at[half, other], dst_ref=gain_recv.at[half, my_row],
            send_sem=gain_send_sem.at[half, step], recv_sem=gain_sem.at[half, step],
            device_id=(other, my_feat), device_id_type=MESH,
        )

    def send_row(step, carry):
        row_copy(nr - step).start()
        return carry

    lax.fori_loop(1, nr, send_row, 0)

    reads[4].wait()

    def pack(block, carry):
        lanes = pl.ds(pl.multiple_of(block * LANES, LANES), LANES)
        for target in range(nr):
            part = bin_ref[target * own : (target + 1) * own, lanes].astype(jnp.float32)
            if own < tile:
                part = jnp.concatenate([part, jnp.zeros((tile - own, LANES), jnp.float32)], axis=0)
            bin_send[target, block] = part.astype(jnp.bfloat16)
        return carry

    lax.fori_loop(0, blocks, pack, 0)

    bin_recv[my_row] = bin_send[my_row]
    acc[...] = jnp.zeros_like(acc)

    row_bytes = pay.at[0, pl.ds(0, nr - 1)]
    feat_bytes = pay.at[pl.ds(0, nf - 1)]
    pltpu.make_async_copy(row_bytes, row_bytes, row_sem).wait()

    def send_feat(step, carry):
        feat_copy(step).start()
        return carry

    lax.fori_loop(1, nf, send_feat, 0)

    def send_bins(place, carry):
        bin_copy(step_of(place, nr)).start()
        return carry

    lax.fori_loop(1, nr, send_bins, 0)
    pltpu.make_async_copy(feat_bytes, feat_bytes, feat_sem).wait()

    def spread(row, carry):
        for feat in range(nf):
            rows = pl.ds((row * nf + feat) * quarter, quarter)
            score[rows, :] = pay[feat, row, 0:quarter, :]
            code[rows, :] = pay[feat, row, quarter : 2 * quarter, :].astype(jnp.int32)
            levelled[rows, :] = pay[feat, row, 2 * quarter : 3 * quarter, :]
        return carry

    lax.fori_loop(0, nr, spread, 0)
    gradient, hessian = cox(score[...], code[...])
    grads[...] = gradient
    hesss[...] = hessian
    mine = pl.ds(me * quarter, quarter)
    grad_ref[...] = grads[mine, :]
    hess_ref[...] = hesss[mine, :]

    levels = lax.broadcasted_iota(jnp.int32, (NODES, LANES), 0).astype(jnp.float32)
    low_levels = [
        (lax.broadcasted_iota(jnp.int32, (16, LANES), 0) + 16 * part).astype(jnp.float32).astype(jnp.bfloat16)
        for part in range(LOW // 16)
    ]
    one = jnp.ones((16, LANES), jnp.bfloat16)
    zero = jnp.zeros((16, LANES), jnp.bfloat16)
    halves = gain_send.shape[0]
    some = own // halves
    width = NODES * some
    short = slice_bins // halves

    def prepare(place, carry):
        step = step_of(place, nr)
        source = partner(my_row, step, nr)

        @pl.when(place > 0)
        def _():
            bin_copy(step).wait_recv()

        for inner in range(blocks):
            block = source * blocks + inner
            row = pl.ds(block, 1)
            is_node = jnp.broadcast_to(levelled[row, :], (NODES, LANES)) == levels
            weight = jnp.concatenate(
                [
                    jnp.where(is_node, jnp.broadcast_to(grads[row, :], (NODES, LANES)), 0.0),
                    jnp.where(is_node, jnp.broadcast_to(hesss[row, :], (NODES, LANES)), 0.0),
                ],
                axis=0,
            )
            weights[block] = weight.astype(jnp.bfloat16)
            bins = bin_recv[source, inner].astype(jnp.float32)
            high = jnp.floor(bins * (1.0 / LOW))
            highs[block] = high
            lows[block] = bins - high * LOW
        count_source(source, 0)
        return carry

    def count_source(source, half):
        def one_chunk(chunk, carry):
            here = [source * blocks + chunk * BLOCKS + inner for inner in range(BLOCKS)]
            weight = [weights[block] for block in here]

            def row_of(ref, block, feature):
                row = ref[block, feature : feature + 1, :]
                return jnp.broadcast_to(row, (16, LANES)).astype(jnp.bfloat16)

            for group in range(half * some // GROUP, (half + 1) * some // GROUP):
                left, right = [], []
                for inner in range(GROUP):
                    feature = group * GROUP + inner
                    high = [row_of(highs, block, feature) for block in here]
                    low = [row_of(lows, block, feature) for block in here]
                    for level in range(HIGH - 1):
                        left.append(
                            jnp.concatenate(
                                [jnp.where(h <= level, w, zero) for h, w in zip(high, weight)], axis=1
                            )
                        )
                    left.append(jnp.concatenate(weight, axis=1))
                    for level in low_levels:
                        right.append(
                            jnp.concatenate([jnp.where(l <= level, one, zero) for l in low], axis=1)
                        )
                acc[group] += lax.dot_general(
                    jnp.concatenate(left, axis=0),
                    jnp.concatenate(right, axis=0),
                    (((1,), (1,)), ((), ())),
                    preferred_element_type=jnp.float32,
                )
            return carry

        lax.fori_loop(0, blocks // BLOCKS, one_chunk, 0)

    def count_again(half, source, carry):
        count_source(source, half)
        return carry

    def send_gain(half, step, carry):
        gain_copy(nr - step, half).start()
        return carry

    def take_gain(half, step, carry):
        gain_copy(step, half).wait_recv()
        return carry

    def split(half):
        for place in range(some):
            group, inner = divmod(half * some + place, GROUP)
            columns = slice(inner * LOW, (inner + 1) * LOW)
            lefts, before, running = [], [None, None], [None, None]
            for level in range(HIGH):
                for stat in range(2):
                    top = ((inner * HIGH + level) * 2 + stat) * NODES
                    part = acc[group, top : top + NODES, columns]
                    lefts.append(running[stat] + (part - before[stat]) if level else part)
                    before[stat] = part
                    running[stat] = jnp.broadcast_to(part[:, LOW - 1 :], (NODES, LOW))
            grad_all, hess_all = running
            base = grad_all * grad_all / (hess_all + 1.0)
            for level in range(HIGH):
                grad_left, hess_left = lefts[2 * level], lefts[2 * level + 1]
                rest = grad_all - grad_left
                gain = (
                    grad_left * grad_left / (hess_left + 1.0)
                    + rest * rest / (hess_all - hess_left + 1.0)
                    - base
                )
                turned[half, level, pl.ds(place, NODES, stride=some), 0:LOW] = gain
        for level in range(HIGH):
            flipped = jnp.transpose(turned[half, level])
            for part in range(LOW // slice_bins):
                top = part * slice_bins
                pieces = [flipped[top + sub * short : top + (sub + 1) * short, :width] for sub in range(halves)]
                whole = jnp.concatenate(pieces, axis=1) if halves > 1 else flipped[top : top + slice_bins]
                gain_send[half, level * (LOW // slice_bins) + part] = whole

    def place_gain(half):
        for source in range(nr):
            for sub in range(halves):
                for node in range(NODES):
                    lanes = sub * width + node * some
                    column = source * own + half * some
                    gain_ref[node, sub * short : (sub + 1) * short, column : column + some] = gain_recv[
                        half, source, :, lanes : lanes + some
                    ]

    for half in range(halves):
        if half:
            lax.fori_loop(0, nr, functools.partial(count_again, half), 0)
        else:
            lax.fori_loop(0, nr, prepare, 0)
        split(half)
        lax.fori_loop(1, nr, functools.partial(send_gain, half), 0)
        gain_recv[half, my_row] = gain_send[half, my_row]
    for half in range(halves):
        lax.fori_loop(1, nr, functools.partial(take_gain, half), 0)
        place_gain(half)

    def settle(step, carry):
        bin_copy(step).wait_send()
        for half in range(halves):
            gain_copy(step, half).wait_send()
        return carry

    lax.fori_loop(1, nr, settle, 0)
    pltpu.make_async_copy(row_bytes, row_bytes, row_send_sem).wait()
    pltpu.make_async_copy(feat_bytes, feat_bytes, feat_send_sem).wait()


def hand_on(*refs):
    count = len(refs) // 3
    sems = refs[-1]
    reads, writes = [], []
    for place in range(count):
        source, target, held = refs[place], refs[count + place], refs[2 * count + place]
        reads.append(pltpu.make_async_copy(source, held, sems.at[0, place]))
        writes.append(pltpu.make_async_copy(held, target, sems.at[1, place]))
    for read in reads:
        read.start()
    for read, write in zip(reads, writes):
        read.wait()
        write.start()
    for write in writes:
        write.wait()


def shards(nr, nf, predictor, events, tie_groups, node_ids, bin_index):
    length = predictor.shape[0]
    quarter = length // LANES
    rows = node_ids.shape[0]
    features = bin_index.shape[0]
    own = features // nr
    blocks = rows // LANES
    tile = -(-own // 16) * 16
    groups = -(-own // GROUP)
    all_rows = nr * blocks
    slice_bins = BINS // nr
    halves = 1
    vmem = pl.BlockSpec(memory_space=pltpu.VMEM)
    f32, bf16 = jnp.float32, jnp.bfloat16
    results = pl.pallas_call(
        functools.partial(kernel, nr, nf),
        out_shape=(
            jax.ShapeDtypeStruct((quarter, LANES), f32),
            jax.ShapeDtypeStruct((quarter, LANES), f32),
            jax.ShapeDtypeStruct((NODES, slice_bins, features), f32),
        ),
        in_specs=[pl.BlockSpec(memory_space=pltpu.HBM)] * 5,
        out_specs=(vmem,) * 3,
        scratch_shapes=[
            pltpu.VMEM((quarter, LANES), f32),
            pltpu.VMEM((quarter, LANES), jnp.int32),
            pltpu.VMEM((quarter, LANES), jnp.int32),
            pltpu.VMEM((blocks, LANES), jnp.int32),
            pltpu.VMEM((features, rows), jnp.int32),
            pltpu.VMEM((all_rows, tile, LANES), f32),
            pltpu.VMEM((all_rows, tile, LANES), f32),
            pltpu.VMEM((all_rows, CHANNELS, LANES), bf16),
            pltpu.VMEM((nf, nr, -(-3 * quarter // 8) * 8, LANES), f32),
            pltpu.VMEM((nr, blocks, tile, LANES), bf16),
            pltpu.VMEM((nr, blocks, tile, LANES), bf16),
            pltpu.VMEM((halves, nr, slice_bins // halves, LANES), f32),
            pltpu.VMEM((halves, nr, slice_bins // halves, LANES), f32),
            pltpu.VMEM((groups, GROUP * HIGH * CHANNELS, GROUP * LOW), f32),
            pltpu.VMEM((halves, HIGH, LANES, LANES), f32),
            pltpu.VMEM((all_rows, LANES), f32),
            pltpu.VMEM((all_rows, LANES), jnp.int32),
            pltpu.VMEM((all_rows, LANES), f32),
            pltpu.VMEM((all_rows, LANES), f32),
            pltpu.VMEM((all_rows, LANES), f32),
            pltpu.SemaphoreType.DMA((5,)),
            pltpu.SemaphoreType.DMA,
            pltpu.SemaphoreType.DMA,
            pltpu.SemaphoreType.DMA,
            pltpu.SemaphoreType.DMA,
            pltpu.SemaphoreType.DMA((nr,)),
            pltpu.SemaphoreType.DMA((nr,)),
            pltpu.SemaphoreType.DMA((halves, nr)),
            pltpu.SemaphoreType.DMA((halves, nr)),
        ],
        compiler_params=pltpu.CompilerParams(
            collective_id=0, has_side_effects=True, vmem_limit_bytes=63 * 1024 * 1024
        ),
    )(
        predictor.reshape(quarter, LANES),
        events.reshape(quarter, LANES),
        tie_groups.reshape(quarter, LANES),
        node_ids.reshape(blocks, LANES),
        bin_index,
    )
    hbm = pl.BlockSpec(memory_space=pltpu.HBM)
    gradient, hessian, gain = pl.pallas_call(
        hand_on,
        out_shape=tuple(jax.ShapeDtypeStruct(a.shape, a.dtype) for a in results),
        in_specs=[hbm] * 3,
        out_specs=(hbm,) * 3,
        scratch_shapes=[pltpu.VMEM(a.shape, a.dtype) for a in results] + [pltpu.SemaphoreType.DMA((2, 3))],
        compiler_params=pltpu.CompilerParams(vmem_limit_bytes=63 * 1024 * 1024),
    )(*results)
    return gradient.reshape(length), hessian.reshape(length), gain.transpose(0, 2, 1)


def solution(mesh):
    return jax.shard_map(
        functools.partial(shards, mesh.shape["row"], mesh.shape["feat"]),
        mesh=mesh,
        in_specs=(
            P(("row", "feat")),
            P(("row", "feat")),
            P(("row", "feat")),
            P("row"),
            P("feat", "row"),
        ),
        out_specs=(P(("row", "feat")), P(("row", "feat")), P(None, "feat", "row")),
        check_vma=False,
    )
```
